128 devices in a mesh: din: 8 (over z, core), dout: 16 (over y, x).
Axes of the slice: x: 4, y: 4, z: 4, core: 2. Of those that a mesh axis runs over, the one named last changes fastest.
Arguments:
- states: bfloat16 [1024, 16384], P(None, 'din'), may hold values from -160 to 160
- lengths: int32 [64], P('din'), may hold values from 1 to 4096, 163840 in all
- norm_gain: float32 [16384], P('din'), may hold values from 0.1 to 1.9
- query_weight: bfloat16 [16384, 16384], P('din', 'dout'), may hold values from -0.046875 to 0.046875
- keyval_weight: bfloat16 [16384, 2048], P('din', 'dout'), may hold values from -0.046875 to 0.046875
- output_weight: bfloat16 [16384, 16384], P('dout', 'din'), may hold values from -0.046875 to 0.046875
- query_scale: float32 [16384], P('dout'), may hold values from 0.5 to 2
- keyval_scale: float32 [2048], P('dout'), may hold values from 1 to 4
- output_scale: float32 [16384], P('din'), may hold values from 8 to 64
- key_cache: bfloat16 [64, 32768, 128], P('din', 'dout'), may hold values from -120 to 120
- value_cache: bfloat16 [64, 32768, 128], P('din', 'dout'), may hold values from -6 to 6
Outputs:
- attended: bfloat16 [1024, 16384], P(None, 'din')
The draws below stay inside these ranges and needn't reach their ends.
Inputs may be any that keep to these rules, and one draw needn't show every extreme that they name: Row r's cache holds keys at positions 0 to lengths[r] - 1; its new tokens take positions lengths[r] onward.
All inputs are finite; a program needn't handle non-finite values. No bound on the sum of `lengths` on one device may be relied on, other than what follows from the above.
Results may differ from the reference program's by a relative error of at most 0.005.
The reference program's roundings to bfloat16 on the way count: a program that leaves them out, or rounds other values in their place, can miss the bound.
Values may be sent and summed in bfloat16 or wider, within the bound.
A program may use at most 128 MiB of HBM per device.

```python
import math
import jax
import jax.numpy as jnp
import numpy as np
from jax import lax

D = 16384
HQ = 128
KVH = 8
HD = 128
CTX = 4096
DRAFT = 16
ROWS = 64
TOKENS = 1024


def draw_states(key, part):
    key = jax.random.fold_in(key, 11)
    key_base, key_rows, key_cols = jax.random.split(key, 3)
    columns = jnp.arange(D, dtype=jnp.float32)
    column_scale = 3.0 ** (columns / D) * jnp.exp(jax.random.uniform(key_cols, (D,)) * math.log(10.0))
    values = jnp.clip(jax.random.normal(key_base, (TOKENS, D)), -4.0, 4.0)
    row_scale = jnp.exp(jax.random.uniform(key_rows, (TOKENS, 1)) * math.log(10.0))
    return (values * row_scale * column_scale * 0.1).astype(jnp.bfloat16)


def draw_key_cache(key, part):
    key = jax.random.fold_in(key, 12)
    key_base = jax.random.fold_in(key, 0)
    shape_full = (ROWS, KVH * CTX, HD)
    values = jnp.clip(jax.random.normal(key_base, shape_full), -5.0, 5.0)
    return values.astype(jnp.bfloat16)


def block_levels(own_key, shape, cuts, low, top_value):
    def one(dim, blocks):
        heights = jax.random.uniform(jax.random.fold_in(jax.random.fold_in(own_key, 6), dim), (blocks,), jnp.float32, low / len(cuts), top_value / len(cuts))
        return jnp.repeat(jnp.exp(heights), shape[dim] // blocks).reshape((-1,) + (1,) * (len(shape) - dim - 1))

    factor_of = one(*cuts[0])
    for cut in cuts[1:]:
        factor_of = factor_of * one(*cut)
    return factor_of


def split_up(count, total, reach, skew):
    weights = [(1 << 20) // math.isqrt(grade ** skew) + 1 for grade in range(2, count + 1)]
    rest, counts = total - reach - (count - 1), [1] * (count - 1)
    while rest > 0:
        movable = [i for i in range(count - 1) if counts[i] < reach]
        pool, budget = sum([weights[i] for i in movable]), rest
        for i in movable:
            more = min(reach - counts[i], max(1, budget * weights[i] // pool), rest)
            counts[i] = counts[i] + more
            rest = rest - more
    return np.array([reach] + counts)


def uneven_parts(rng, count, total, limit, skew):
    if count == 2:
        one = jax.random.randint(rng, (), max(1, total - limit), min(limit, total - 1) + 1)
        return jnp.stack([one, total - one])
    tallies = jnp.asarray(split_up(count, total, limit, skew), jnp.int32)
    couples = (count - 1) // 2
    giver, receiver = tallies[1:1 + 2 * couples:2], tallies[2:2 + 2 * couples:2]
    room = jnp.minimum(giver - 1, limit - receiver)
    moved = jax.random.randint(jax.random.fold_in(rng, 1), (couples,), 0, 1 << 20) % (room + 1)
    tallies = tallies.at[1:1 + 2 * couples:2].set(giver - moved).at[2:2 + 2 * couples:2].set(receiver + moved)
    return tallies[jax.random.permutation(jax.random.fold_in(rng, 2), count)]


def centred(stream_key, dims, scale, most, pieces=(), held_as=jnp.bfloat16):
    drawn = scale * jax.random.normal(stream_key, dims, jnp.float32)
    if pieces:
        drawn = drawn * block_levels(stream_key, dims, pieces, -0.22, 0.18)
    return jnp.clip(drawn, -most, most).astype(held_as)


def setup_inputs(seed: int = 0) -> dict:
    splits = jax.random.split(jax.random.key(seed), 12)
    states = draw_states(jax.random.fold_in(splits[11], 71), 0)
    lengths = uneven_parts(splits[1], ROWS, ROWS * CTX * 5 // 8, CTX, 1).astype(jnp.int32)
    norm_gain = jnp.clip(1.0 + 0.18 * jax.random.normal(splits[2], (D,), jnp.float32), 0.1, 1.9)
    query_weight = centred(splits[3], (D, HQ * HD), D ** -0.5, 0.046875, ((0, 8), (1, 16)))
    keyval_weight = centred(splits[4], (D, 2 * KVH * HD), D ** -0.5, 0.046875, ((0, 8), (1, 16)))
    output_weight = centred(splits[5], (HQ * HD, D), (HQ * HD) ** -0.5, 0.046875, ((0, 16), (1, 8)))
    query_scale = jnp.clip(jnp.exp(math.log(2.0) - 1.3862944 * jax.random.uniform(splits[6], (HQ * HD,), jnp.float32) ** block_levels(splits[6], (HQ * HD,), ((0, 16),), -0.2, 0.2)), 0.5, 2.0)
    keyval_scale = jnp.clip(jnp.exp(math.log(4.0) - 1.3862944 * jax.random.uniform(splits[7], (2 * KVH * HD,), jnp.float32) ** block_levels(splits[7], (2 * KVH * HD,), ((0, 16),), -0.2, 0.2)), 1.0, 4.0)
    output_scale = jnp.clip(jnp.exp(math.log(64.0) - 2.0794415 * jax.random.uniform(splits[8], (D,), jnp.float32) ** block_levels(splits[8], (D,), ((0, 8),), -0.2, 0.2)), 8.0, 64.0)
    key_cache = draw_key_cache(jax.random.fold_in(splits[11], 71), 0)
    value_cache = centred(splits[10], (ROWS, KVH * CTX, HD), 1.0, 6.0, ((0, 8), (1, 16)))
    return dict(states=states, lengths=lengths, norm_gain=norm_gain, query_weight=query_weight, keyval_weight=keyval_weight, output_weight=output_weight, query_scale=query_scale, keyval_scale=keyval_scale, output_scale=output_scale, key_cache=key_cache, value_cache=value_cache)


def rotary_table(head_size):
    entries = []
    for index in range(head_size // 2):
        inverse = 1.0 / 500000.0 ** (2.0 * index / head_size)
        wavelength = 2.0 * math.pi / inverse
        smooth = min(max((8192.0 / wavelength - 1.0) / 3.0, 0.0), 1.0)
        entries.append((1.0 - smooth) * inverse / 8.0 + smooth * inverse)
    return jnp.asarray(entries, dtype=jnp.float32)

def rotate(vectors, cosine, sine_part):
    halfway = vectors.shape[-1] // 2
    former = vectors[..., :halfway]
    latter = vectors[..., halfway:]
    return jnp.concatenate([former * cosine - latter * sine_part, latter * cosine + former * sine_part], axis=-1)

def one_row(packed):
    query_row, key_row, value_row, cache_keys, cache_values, length_row = packed
    factor = 1.0 / math.sqrt(query_row.shape[-1])
    span = cache_keys.shape[1]
    count = query_row.shape[0]
    query_wide = query_row.astype(jnp.float32)
    cached = jnp.einsum('tkgd,kpd->kgtp', query_wide, cache_keys.astype(jnp.float32), precision=lax.Precision.HIGHEST) * factor
    drafted = jnp.einsum('tkgd,ukd->kgtu', query_wide, key_row.astype(jnp.float32), precision=lax.Precision.HIGHEST) * factor
    cache_valid = (jnp.arange(span, dtype=jnp.int32) < length_row)[None, None, None, :]
    draft_steps = jnp.arange(count, dtype=jnp.int32)
    draft_valid = (draft_steps[None, :] <= draft_steps[:, None])[None, None, :, :]
    cached = jnp.where(cache_valid, cached, -1e+30)
    drafted = jnp.where(draft_valid, drafted, -1e+30)
    highest = jnp.maximum(lax.optimization_barrier(jnp.max(cached, axis=3, keepdims=True)), lax.optimization_barrier(jnp.max(drafted, axis=3, keepdims=True)))
    cache_weights = jnp.where(cache_valid, jnp.exp(cached - highest), 0.0)
    draft_weights = jnp.where(draft_valid, jnp.exp(drafted - highest), 0.0)
    totals = lax.optimization_barrier(jnp.sum(cache_weights, axis=3, keepdims=True)) + lax.optimization_barrier(jnp.sum(draft_weights, axis=3, keepdims=True))
    rounded_cache = lax.optimization_barrier(cache_weights.astype(jnp.bfloat16)).astype(jnp.float32)
    rounded_draft = lax.optimization_barrier(draft_weights.astype(jnp.bfloat16)).astype(jnp.float32)
    weighted = jnp.einsum('kgtp,kpd->kgtd', rounded_cache, cache_values.astype(jnp.float32), precision=lax.Precision.HIGHEST)
    weighted = weighted + jnp.einsum('kgtu,ukd->kgtd', rounded_draft, value_row.astype(jnp.float32), precision=lax.Precision.HIGHEST)
    heads_out = weighted / totals
    return jnp.transpose(heads_out, (2, 0, 1, 3)).reshape(count, -1).astype(jnp.bfloat16)

def reference(states, lengths, norm_gain, query_weight, keyval_weight, output_weight, query_scale, keyval_scale, output_scale, key_cache, value_cache):
    widened = states.astype(jnp.float32)
    inverse = lax.rsqrt(lax.optimization_barrier(jnp.sum(widened * widened, axis=1)) / D + 1e-05)
    scaled = (widened * norm_gain).astype(jnp.bfloat16)
    queries_raw = jnp.dot(scaled, query_weight, preferred_element_type=jnp.float32) * query_scale * inverse[:, None]
    pairs_raw = jnp.dot(scaled, keyval_weight, preferred_element_type=jnp.float32) * keyval_scale * inverse[:, None]
    positions = (lengths[:, None] + jnp.arange(DRAFT, dtype=jnp.int32)[None, :]).reshape(TOKENS)
    angles = positions.astype(jnp.float32)[:, None] * rotary_table(HD)[None, :]
    cosine = jnp.cos(angles)[:, None, :]
    sine_part = jnp.sin(angles)[:, None, :]
    queries = rotate(queries_raw.reshape(TOKENS, HQ, HD), cosine, sine_part).astype(jnp.bfloat16)
    pairs = pairs_raw.reshape(TOKENS, KVH, 2, HD)
    new_keys = rotate(pairs[:, :, 0, :], cosine, sine_part).astype(jnp.bfloat16)
    new_values = pairs[:, :, 1, :].astype(jnp.bfloat16)
    group = HQ // KVH
    query_rows = queries.reshape(ROWS, DRAFT, KVH, group, HD)
    key_rows = new_keys.reshape(ROWS, DRAFT, KVH, HD)
    value_rows = new_values.reshape(ROWS, DRAFT, KVH, HD)
    cache_keys = key_cache.reshape(ROWS, KVH, CTX, HD)
    cache_values = value_cache.reshape(ROWS, KVH, CTX, HD)
    attention = lax.map(one_row, (query_rows, key_rows, value_rows, cache_keys, cache_values, lengths))
    attention = attention.reshape(TOKENS, HQ * HD)
    return (jnp.dot(attention, output_weight, preferred_element_type=jnp.float32) * output_scale).astype(jnp.bfloat16)
```

```python
import functools
import math

import jax
import jax.numpy as jnp
from jax import lax
from jax.experimental import pallas as pl
from jax.experimental.pallas import tpu as pltpu
from jax.sharding import PartitionSpec as P

D = 16384
HQ = 128
KVH = 8
HD = 128
DRAFT = 16
ROWS_HERE = 8
OWN = 8
QW = OWN * HD
WIDE = QW + 2 * HD
SPAN = 2048
FEATS = 2048
OUTS = 2048

CHUNK_ROWS = 2
NC = ROWS_HERE // CHUNK_ROWS
T = CHUNK_ROWS * DRAFT
NB = 8
M = NB * T
LOG_SCALE = math.log2(math.e) / math.sqrt(HD)
LOWEST = -1e30

CORE = 0
ZRS = 1
SWAP = 7
FAR = 9
ZAG = FAR + CHUNK_ROWS
CAG = ZAG + 4
RS1 = CAG + 4
RS2 = RS1 + 12
AG2 = RS2 + 12
AG1 = AG2 + 8
NSEM = AG1 + 8


def rotary_table(head_size):
    entries = []
    for index in range(head_size // 2):
        inverse = 1.0 / 500000.0 ** (2.0 * index / head_size)
        wavelength = 2.0 * math.pi / inverse
        smooth = min(max((8192.0 / wavelength - 1.0) / 3.0, 0.0), 1.0)
        entries.append((1.0 - smooth) * inverse / 8.0 + smooth * inverse)
    return jnp.asarray(entries, dtype=jnp.float32)


def mod4(v):
    return lax.rem(v, 4)


def f32(v):
    return v.astype(jnp.float32)


def kernel(
    lengths, gain, qscale, kvscale, oscale, cosines, sines,
    states, wq, wkv, wo, keys, values,
    out,
    xs, wq_v, wkv_v, wo_v, k_v, v_v, scaled,
    ybuf, crecv, zrecv, qbuf, kvbuf, kpad, vpad, obuf, orecv, gat,
    pbuf, r1, gf, gb, r2, outb,
    load_sem, send_sem, recv_sem, store_sem,
):
    din = lax.axis_index("din")
    dout = lax.axis_index("dout")
    core = lax.rem(din, 2)
    z = lax.div(din, 2)
    x = lax.rem(dout, 4)
    y = lax.div(dout, 4)
    parity = lax.rem(x, 2)
    core_peer = (din + 1 - 2 * core, dout)
    pair_peer = (din, dout + 1 - 2 * parity)
    z_plus = (lax.rem(din + 2, 8), dout)
    z_minus = (lax.rem(din + 6, 8), dout)
    x_plus = (din, 4 * y + mod4(x + 1))
    x_minus = (din, 4 * y + mod4(x + 3))
    y_plus = (din, lax.rem(dout + 4, 16))
    y_minus = (din, lax.rem(dout + 12, 16))
    neighbours = (core_peer, z_plus, z_minus, x_plus, x_minus, y_plus, y_minus)

    def load(src, dst, index):
        return pltpu.make_async_copy(src, dst, load_sem.at[index])

    def states_load(c):
        return load(states.at[:, pl.ds(c * T, T), :], xs.at[c], c)

    wq_load = load(wq, wq_v, NC)
    wkv_load = load(wkv, wkv_v, NC + 1)
    wo_load = load(wo, wo_v, NC + 2)
    k_load = load(keys, k_v, NC + 3)
    v_load = load(values, v_v, NC + 4)
    states_load(0).start()
    wq_load.start()
    wkv_load.start()
    for c in range(1, NC):
        states_load(c).start()
    k_load.start()
    v_load.start()
    wo_load.start()

    barrier = pltpu.get_barrier_semaphore()
    for peer in neighbours:
        pl.semaphore_signal(barrier, inc=1, device_id=peer, device_id_type=pl.DeviceIdType.MESH)
    pl.semaphore_wait(barrier, len(neighbours))

    started = []

    def remote(src, dst, row, c, peer):
        return pltpu.make_async_remote_copy(
            src_ref=src,
            dst_ref=dst,
            send_sem=send_sem.at[row, c],
            recv_sem=recv_sem.at[row, c],
            device_id=peer,
            device_id_type=pl.DeviceIdType.MESH,
        )

    def send(src, dst, row, c, peer):
        copy = remote(src, dst, row, c, peer)
        copy.start()
        started.append(copy)

    def arrived(dst, row, c):
        remote(dst, dst, row, c, core_peer).wait_recv()

    def scatter_start(base, c, shard, land, index, plus, minus):
        far = mod4(index + 2)
        send(shard(far, 1), land(0), base, c, plus)
        send(shard(far, 0), land(1), base + 1, c, minus)
        send(shard(mod4(index + 1), 0), land(2), base + 2, c, plus)
        send(shard(mod4(index + 3), 1), land(3), base + 3, c, minus)

    def scatter_mid(base, c, shard, land, index, plus, minus, own=None):
        own = own or shard
        for slot, step, half, peer in ((0, 1, 1, plus), (1, 3, 0, minus)):
            target = mod4(index + step)
            arrived(land(slot), base + slot, c)
            piece = shard(target, half)
            piece[...] = (f32(own(target, half)[...]) + f32(land(slot)[...])).astype(piece.dtype)
            send(piece, land(4 + slot), base + 4 + slot, c, peer)

    def scatter_end(base, c, shard, land, index):
        halves = []
        for half, direct, chained in ((0, 2, 5), (1, 3, 4)):
            arrived(land(direct), base + direct, c)
            arrived(land(chained), base + chained, c)
            halves.append(
                f32(shard(index, half)[...]) + f32(land(direct)[...]) + f32(land(chained)[...])
            )
        return halves

    def gather_start(base, c, part, index, plus, minus):
        own = part(index, None)
        send(own, own, base, c, plus)
        send(own, own, base + 1, c, minus)

    def gather_mid(base, c, part, index, plus, minus):
        for slot, step, half, peer in ((0, 3, 0, plus), (1, 1, 1, minus)):
            source = mod4(index + step)
            arrived(part(source, None), base + slot, c)
            piece = part(source, half)
            send(piece, piece, base + 2 + slot, c, peer)

    def gather_end(base, c, part, index):
        far = mod4(index + 2)
        arrived(part(far, 0), base + 2, c)
        arrived(part(far, 1), base + 3, c)

    def z_shard(c):
        return lambda t, h: ybuf.at[c, core, t, pl.ds(h * (T // 2), T // 2), :]

    def z_land(c):
        return lambda slot: zrecv.at[c, slot]

    def project(c):
        states_load(c).wait()
        wide = f32(xs[c]).reshape(M, FEATS)
        squares = jnp.sum(wide * wide, axis=1, keepdims=True)
        scaled[...] = (wide * gain[...]).astype(jnp.bfloat16)
        if c == 0:
            wq_load.wait()
            wkv_load.wait()

        def put(block, start):
            for b in range(NB):
                ybuf[c, b % 2, b // 2, :, start] = block[b * T : (b + 1) * T]

        put(jnp.broadcast_to(squares, (M, HD)), pl.ds(QW + HD, HD))
        put(
            jnp.dot(scaled[...], wkv_v[...], preferred_element_type=jnp.float32), pl.ds(QW, HD)
        )

        @pl.loop(0, QW // 256)
        def _(j):
            start = pl.ds(pl.multiple_of(j * 256, 256), 256)
            put(
                jnp.dot(scaled[...], wq_v[:, start], preferred_element_type=jnp.float32), start
            )

        send(ybuf.at[c, 1 - core], crecv.at[c], CORE, c, core_peer)

    def pair_cores(c):
        arrived(crecv.at[c], CORE, c)
        ybuf[c, core] = ybuf[c, core] + crecv[c]
        scatter_start(ZRS, c, z_shard(c), z_land(c), z, z_plus, z_minus)

    def project_mid(c):
        scatter_mid(ZRS, c, z_shard(c), z_land(c), z, z_plus, z_minus)

    def project_end(c):
        total = jnp.concatenate(scatter_end(ZRS, c, z_shard(c), z_land(c), z), axis=0)
        inverse = lax.rsqrt(total[:, QW + HD :] / D + 1e-05)
        cosine = cosines[c]
        sine = sines[c]
        half = HD // 2
        for h in range(OWN):
            cols = slice(h * HD, (h + 1) * HD)
            raw = total[:, cols] * qscale[:, cols] * inverse
            turned = jnp.concatenate([raw[:, half:], raw[:, :half]], axis=1)
            query = (raw * cosine + turned * sine).astype(jnp.bfloat16)
            for r in range(CHUNK_ROWS):
                qbuf[c, parity, r, pl.ds(h * DRAFT, DRAFT), :] = query[
                    r * DRAFT : (r + 1) * DRAFT
                ]
        raw = total[:, QW : QW + HD] * kvscale[...] * inverse
        turned = jnp.concatenate([raw[:, half:], raw[:, :half]], axis=1)
        rotated = raw * cosine + turned * sine
        kvbuf[c, parity] = jnp.where(parity == 0, rotated, raw).astype(jnp.bfloat16)
        send(qbuf.at[c, parity], qbuf.at[c, parity], SWAP, c, pair_peer)
        send(kvbuf.at[c, parity], kvbuf.at[c, parity], SWAP + 1, c, pair_peer)

    def attend(c):
        if c == 0:
            kpad[...] = jnp.zeros_like(kpad)
            vpad[...] = jnp.zeros_like(vpad)
            k_load.wait()
            v_load.wait()
        arrived(qbuf.at[c, 1 - parity], SWAP, c)
        arrived(kvbuf.at[c, 1 - parity], SWAP + 1, c)
        place = lax.broadcasted_iota(jnp.int32, (1, SPAN), 1) + parity * SPAN
        token = lax.rem(lax.broadcasted_iota(jnp.int32, (2 * OWN * DRAFT, HD), 0), DRAFT)
        other = lax.broadcasted_iota(jnp.int32, (2 * OWN * DRAFT, HD), 1)
        drafted = (other <= token) & (parity == 0)
        lane = lax.broadcasted_iota(jnp.int32, (QW // OWN, HD), 1)
        for r in range(CHUNK_ROWS):
            row = c * CHUNK_ROWS + r
            kpad[0:DRAFT] = kvbuf[c, 0, r * DRAFT : (r + 1) * DRAFT]
            vpad[0:DRAFT] = kvbuf[c, 1, r * DRAFT : (r + 1) * DRAFT]
            query = jnp.concatenate([qbuf[c, 0, r], qbuf[c, 1, r]], axis=0)
            across = (((1,), (1,)), ((), ()))
            bias = jnp.where(place < lengths[row], 0.0, LOWEST)
            scores = (
                lax.dot_general(query, k_v[row], across, preferred_element_type=jnp.float32)
                * LOG_SCALE
                + bias
            )
            fresh = lax.dot_general(query, kpad[...], across, preferred_element_type=jnp.float32)
            fresh = jnp.where(drafted, fresh * LOG_SCALE, LOWEST)
            top = jnp.maximum(
                jnp.max(scores, axis=1, keepdims=True), jnp.max(fresh, axis=1, keepdims=True)
            )
            weights = jnp.exp2(scores - top)
            fresh_weights = jnp.exp2(fresh - top)
            totals = jnp.sum(weights, axis=1, keepdims=True) + jnp.sum(
                fresh_weights, axis=1, keepdims=True
            )
            weighted = jnp.dot(
                weights.astype(jnp.bfloat16), v_v[row], preferred_element_type=jnp.float32
            ) + jnp.dot(
                fresh_weights.astype(jnp.bfloat16), vpad[...], preferred_element_type=jnp.float32
            )
            for p in range(2):
                mine = slice(p * QW // OWN, (p + 1) * QW // OWN)
                both = jnp.where(lane < HD // 2, top[mine], totals[mine]).T
                obuf[c, p, r, 0:HD] = weighted[mine]
                obuf[c, p, r, HD : HD + 8] = both[0:8]
                obuf[c, p, r, HD + 8 : HD + 16] = both[HD // 2 : HD // 2 + 8]
            send(obuf.at[c, 1 - parity, r], orecv.at[c, r], FAR + r, c, pair_peer)

    def att_part(c):
        def part(t, half):
            if half is None:
                return gat.at[c, 2 * t + core]
            return gat.at[c, 2 * t + core, :, pl.ds(half * (QW // 2), QW // 2)]

        return part

    def to_core(c, slot, t):
        block = gat.at[c, 2 * t + core]
        send(block, block, CAG + slot, c, core_peer)

    def combine(c):
        for r in range(CHUNK_ROWS):
            arrived(orecv.at[c, r], FAR + r, c)
            near_top = obuf[c, parity, r, HD : HD + 8]
            near_total = obuf[c, parity, r, HD + 8 : HD + 16]
            far_top = orecv[c, r, HD : HD + 8]
            far_total = orecv[c, r, HD + 8 : HD + 16]
            joint = jnp.maximum(near_top, far_top)
            near_factor = jnp.exp2(near_top - joint)
            far_factor = jnp.exp2(far_top - joint)
            share = 1.0 / (near_total * near_factor + far_total * far_factor)

            def spread(factor):
                return jnp.broadcast_to((factor * share)[0:1], (HD, HD)).T

            heads = (
                obuf[c, parity, r, 0:HD] * spread(near_factor)
                + orecv[c, r, 0:HD] * spread(far_factor)
            ).astype(jnp.bfloat16)
            for h in range(OWN):
                gat[c, din, r * DRAFT : (r + 1) * DRAFT, h * HD : (h + 1) * HD] = heads[
                    h * DRAFT : (h + 1) * DRAFT
                ]
        gather_start(ZAG, c, att_part(c), z, z_plus, z_minus)
        to_core(c, 0, z)

    def gather_heads(c):
        gather_mid(ZAG, c, att_part(c), z, z_plus, z_minus)
        to_core(c, 1, mod4(z + 3))
        to_core(c, 2, mod4(z + 1))

    def gather_far_heads(c):
        gather_end(ZAG, c, att_part(c), z)
        to_core(c, 3, mod4(z + 2))

    first = ((x, x_plus, x_minus), (y, y_plus, y_minus))
    second = ((y, y_plus, y_minus), (x, x_plus, x_minus))

    def columns(side, t):
        return pl.ds(pl.multiple_of(side * (OUTS // 2) + t * 256, 256), 256)

    def shard1(c, side):
        return lambda t, h: pbuf.at[c, pl.ds(h * 4, 4), :, columns(side, t)]

    def land1(c, side):
        return lambda slot: r1.at[c, side, slot]

    def shard2(c, side, buffer):
        return lambda t, h: buffer.at[c, side, 2 * t + h]

    def land2(c, side):
        return lambda slot: r2.at[c, side, slot]

    def part2(c, side):
        def part(t, half):
            place = columns(side, first[side][0])
            if half is None:
                return outb.at[c, pl.ds(2 * t, 2), :, place]
            return outb.at[c, pl.ds(2 * t + half, 1), :, place]

        return part

    def part1(c, side):
        def part(t, half):
            if half is None:
                return outb.at[c, :, :, columns(side, t)]
            return outb.at[c, pl.ds(half * 4, 4), :, columns(side, t)]

        return part

    def output(c):
        if c == 0:
            wo_load.wait()
        for slot, step in enumerate((0, 3, 1, 2)):
            t = mod4(z + step)
            arrived(gat.at[c, 2 * t + 1 - core], CAG + slot, c)

        @pl.loop(0, OUTS // 256)
        def _(j):
            cols = pl.ds(pl.multiple_of(j * 256, 256), 256)
            block = jnp.dot(
                gat[c].reshape(M, QW), wo_v[:, cols], preferred_element_type=jnp.float32
            )
            pbuf[c, :, :, cols] = block.astype(jnp.bfloat16).reshape(NB, T, 256)

        for side in range(2):
            scatter_start(RS1 + 6 * side, c, shard1(c, side), land1(c, side), *first[side])

    def sum_mid(c):
        for side in range(2):
            scatter_mid(RS1 + 6 * side, c, shard1(c, side), land1(c, side), *first[side])

    def sum_end(c):
        for side in range(2):
            halves = scatter_end(
                RS1 + 6 * side, c, shard1(c, side), land1(c, side), first[side][0]
            )
            for h in range(2):
                gf[c, side, h * 4 : (h + 1) * 4] = halves[h]
                gb[c, side, h * 4 : (h + 1) * 4] = halves[h].astype(jnp.bfloat16)
            scatter_start(
                RS2 + 6 * side, c, shard2(c, side, gb), land2(c, side), *second[side]
            )

    def cross_mid(c):
        for side in range(2):
            scatter_mid(
                RS2 + 6 * side,
                c,
                shard2(c, side, gb),
                land2(c, side),
                *second[side],
                own=shard2(c, side, gf),
            )

    def cross_end(c):
        for side in range(2):
            index = second[side][0]
            halves = scatter_end(
                RS2 + 6 * side, c, shard2(c, side, gf), land2(c, side), index
            )
            cols = columns(side, first[side][0])
            for h in range(2):
                outb[c, 2 * index + h, :, cols] = (halves[h] * oscale[:, cols]).astype(
                    jnp.bfloat16
                )
            gather_start(AG2 + 4 * side, c, part2(c, side), *second[side])

    def spread_mid(c):
        for side in range(2):
            gather_mid(AG2 + 4 * side, c, part2(c, side), *second[side])

    def spread_end(c):
        for side in range(2):
            gather_end(AG2 + 4 * side, c, part2(c, side), second[side][0])
            gather_start(AG1 + 4 * side, c, part1(c, side), *first[side])

    def last_mid(c):
        for side in range(2):
            gather_mid(AG1 + 4 * side, c, part1(c, side), *first[side])

    def out_store(c):
        return pltpu.make_async_copy(
            outb.at[c], out.at[:, pl.ds(c * T, T), :], store_sem.at[c]
        )

    def last_end(c):
        for side in range(2):
            gather_end(AG1 + 4 * side, c, part1(c, side), first[side][0])
        out_store(c).start()

    stages = (
        (project, 0.0, 1.6),
        (pair_cores, 1.8, 2.0),
        (project_mid, 6.0, 5.0),
        (project_end, 8.5, 5.0),
        (attend, 11.0, 5.5),
        (combine, 14.0, 5.5),
        (gather_heads, 16.5, 5.5),
        (gather_far_heads, 18.5, 5.5),
        (output, 20.0, 9.0),
        (sum_mid, 23.5, 9.6),
        (sum_end, 26.0, 9.6),
        (cross_mid, 28.0, 9.6),
        (cross_end, 30.0, 9.6),
        (spread_mid, 32.0, 9.6),
        (spread_end, 34.0, 9.6),
        (last_mid, 37.0, 9.6),
        (last_end, 40.0, 9.6),
    )
    order = sorted(
        (begin + c * gap, i, c) for i, (_, begin, gap) in enumerate(stages) for c in range(NC)
    )
    for _, i, c in order:
        stages[i][0](c)

    for c in range(NC):
        out_store(c).wait()
    for copy in started:
        copy.wait_send()


def shards(
    states,
    lengths,
    norm_gain,
    query_weight,
    keyval_weight,
    output_weight,
    query_scale,
    keyval_scale,
    output_scale,
    key_cache,
    value_cache,
):
    positions = (lengths[:, None] + jnp.arange(DRAFT, dtype=jnp.int32)[None, :]).reshape(NC, T, 1)
    angles = positions.astype(jnp.float32) * rotary_table(HD)
    cosine = jnp.cos(angles)
    sine = jnp.sin(angles)
    cosines = jnp.concatenate([cosine, cosine], axis=2)
    sines = jnp.concatenate([-sine, sine], axis=2)
    bf16 = jnp.bfloat16
    vmem = pl.BlockSpec(memory_space=pltpu.VMEM)
    smem = pl.BlockSpec(memory_space=pltpu.SMEM)
    hbm = pl.BlockSpec(memory_space=pl.ANY)
    result = pl.pallas_call(
        kernel,
        out_shape=jax.ShapeDtypeStruct((NB, ROWS_HERE * DRAFT, OUTS), bf16),
        in_specs=[smem] + [vmem] * 6 + [hbm] * 6,
        out_specs=hbm,
        scratch_shapes=[
            pltpu.VMEM((NC, NB, T, FEATS), bf16),
            pltpu.VMEM((FEATS, QW), bf16),
            pltpu.VMEM((FEATS, HD), bf16),
            pltpu.VMEM((QW, OUTS), bf16),
            pltpu.VMEM((ROWS_HERE, SPAN, HD), bf16),
            pltpu.VMEM((ROWS_HERE, SPAN, HD), bf16),
            pltpu.VMEM((M, FEATS), bf16),
            pltpu.VMEM((NC, 2, 4, T, WIDE), jnp.float32),
            pltpu.VMEM((NC, 4, T, WIDE), jnp.float32),
            pltpu.VMEM((NC, 6, T // 2, WIDE), jnp.float32),
            pltpu.VMEM((NC, 2, CHUNK_ROWS, OWN * DRAFT, HD), bf16),
            pltpu.VMEM((NC, 2, T, HD), bf16),
            pltpu.VMEM((HD, HD), bf16),
            pltpu.VMEM((HD, HD), bf16),
            pltpu.VMEM((NC, 2, CHUNK_ROWS, HD + 16, HD), jnp.float32),
            pltpu.VMEM((NC, CHUNK_ROWS, HD + 16, HD), jnp.float32),
            pltpu.VMEM((NC, NB, T, QW), bf16),
            pltpu.VMEM((NC, NB, T, OUTS), bf16),
            pltpu.VMEM((NC, 2, 6, 4, T, 256), bf16),
            pltpu.VMEM((NC, 2, NB, T, 256), jnp.float32),
            pltpu.VMEM((NC, 2, NB, T, 256), bf16),
            pltpu.VMEM((NC, 2, 6, T, 256), bf16),
            pltpu.VMEM((NC, NB, T, OUTS), bf16),
            pltpu.SemaphoreType.DMA((NC + 5,)),
            pltpu.SemaphoreType.DMA((NSEM, NC)),
            pltpu.SemaphoreType.DMA((NSEM, NC)),
            pltpu.SemaphoreType.DMA((NC,)),
        ],
        compiler_params=pltpu.CompilerParams(
            collective_id=0, has_side_effects=True, vmem_limit_bytes=63 * 2**20
        ),
        cost_estimate=pl.CostEstimate(
            flops=12 * 10**9, bytes_accessed=25 * 2**20, transcendentals=2**22
        ),
    )(
        lengths,
        norm_gain[None, :],
        query_scale[None, :],
        keyval_scale[None, :],
        output_scale[None, :],
        cosines,
        sines,
        states.reshape(NB, ROWS_HERE * DRAFT, FEATS),
        query_weight,
        keyval_weight,
        output_weight,
        key_cache,
        value_cache,
    )
    return result.reshape(NB * ROWS_HERE * DRAFT, OUTS)


def solution(mesh):
    placed = (
        P(None, "din"),
        P("din"),
        P("din"),
        P("din", "dout"),
        P("din", "dout"),
        P("dout", "din"),
        P("dout"),
        P("dout"),
        P("din"),
        P("din", "dout", None),
        P("din", "dout", None),
    )
    return jax.shard_map(
        shards, mesh=mesh, in_specs=placed, out_specs=P(None, "din"), check_vma=False
    )
```

```python
import functools
import math

import jax
import jax.numpy as jnp
from jax import lax
from jax.experimental import pallas as pl
from jax.experimental.pallas import tpu as pltpu
from jax.sharding import PartitionSpec as P

D = 16384
HQ = 128
KVH = 8
HD = 128
DRAFT = 16
ROWS_HERE = 8
OWN = 8
QW = OWN * HD
WIDE = QW + 2 * HD
SPAN = 2048
TILE = 512
FEATS = 2048
OUTS = 2048

CHUNK_ROWS = 2
NC = ROWS_HERE // CHUNK_ROWS
T = CHUNK_ROWS * DRAFT
NB = 8
M = NB * T
LOG_SCALE = math.log2(math.e) / math.sqrt(HD)
LOWEST = -1e30
LIMIT = 56

WIDTH = OUTS // 8

CORE = 0
ZRS = 1
SWAP = 7
FAR = 9
ZAG = FAR + CHUNK_ROWS
CAG = ZAG + 3
RS1 = CAG + 4
RS2 = RS1 + 12
AG2 = RS2 + 6
AG1 = AG2 + 6
NSEM = AG1 + 8

ORDER = (
    (0, 0), (1, 0), (0, 1), (3, 0), (1, 1), (0, 2), (2, 0), (1, 2), (2, 1), (0, 3),
    (1, 3), (2, 2), (3, 1), (0, 4), (2, 3), (3, 2), (1, 4), (0, 5), (3, 3), (2, 4),
    (1, 5), (0, 6), (3, 4), (0, 7), (2, 5), (1, 6), (1, 7), (3, 5), (2, 6), (0, 8),
    (1, 8), (2, 7), (3, 6), (0, 9), (3, 7), (2, 8), (1, 9), (0, 10), (3, 8), (2, 9),
    (1, 10), (0, 11), (3, 9), (1, 11), (2, 10), (3, 10), (1, 12), (2, 11), (1, 13), (3, 11),
    (2, 12), (0, 12), (3, 12), (0, 13), (2, 13), (3, 13),
)


def rotary_table(head_size):
    entries = []
    for index in range(head_size // 2):
        inverse = 1.0 / 500000.0 ** (2.0 * index / head_size)
        wavelength = 2.0 * math.pi / inverse
        smooth = min(max((8192.0 / wavelength - 1.0) / 3.0, 0.0), 1.0)
        entries.append((1.0 - smooth) * inverse / 8.0 + smooth * inverse)
    return jnp.asarray(entries, dtype=jnp.float32)


def mod4(v):
    return lax.rem(v, 4)


def f32(v):
    return v.astype(jnp.float32)


def kernel(
    lengths, frequencies, gain, qscale, kvscale, oscale,
    states, wq, wkv, wo, keys, values,
    out,
    cosines, sines,
    xs, wq_v, wkv_v, wo_v, k_v, v_v, scaled,
    ybuf, crecv, zrecv, qbuf, kvbuf, kpad, vpad, obuf, orecv, gat,
    pbuf,
    load_sem, send_sem, recv_sem,
    *sides,
):
    r1, gf, gb, r2 = (
        [[sides[4 * (2 * c + side) + kind] for side in range(2)] for c in range(NC)]
        for kind in range(4)
    )
    din = lax.axis_index("din")
    dout = lax.axis_index("dout")
    core = lax.rem(din, 2)
    z = lax.div(din, 2)
    x = lax.rem(dout, 4)
    y = lax.div(dout, 4)
    parity = lax.rem(x, 2)
    core_peer = (din + 1 - 2 * core, dout)
    pair_peer = (din, dout + 1 - 2 * parity)
    z_plus = (lax.rem(din + 2, 8), dout)
    z_minus = (lax.rem(din + 6, 8), dout)
    x_plus = (din, 4 * y + mod4(x + 1))
    x_minus = (din, 4 * y + mod4(x + 3))
    y_plus = (din, lax.rem(dout + 4, 16))
    y_minus = (din, lax.rem(dout + 12, 16))
    z_ring = (z_plus, (lax.rem(din + 4, 8), dout), z_minus)
    x_ring = (x_plus, (din, 4 * y + mod4(x + 2)), x_minus)
    y_ring = (y_plus, (din, lax.rem(dout + 8, 16)), y_minus)
    neighbours = (core_peer, *z_ring, *x_ring, *y_ring)

    def load(src, dst, index):
        return pltpu.make_async_copy(src, dst, load_sem.at[index])

    def states_load(c):
        return load(states.at[:, pl.ds(c * T, T), :], xs.at[c], c)

    wq_load = load(wq, wq_v, NC)
    wkv_load = load(wkv, wkv_v, NC + 1)
    wo_load = load(wo, wo_v, NC + 2)
    k_load = load(keys, k_v, NC + 3)
    v_load = load(values, v_v, NC + 4)
    states_load(0).start()
    wq_load.start()
    wkv_load.start()
    for c in range(1, NC):
        states_load(c).start()
    k_load.start()
    v_load.start()
    wo_load.start()

    draft = lax.broadcasted_iota(jnp.int32, (DRAFT, HD), 0)
    sign = jnp.where(lax.broadcasted_iota(jnp.int32, (DRAFT, HD), 1) < HD // 2, -1.0, 1.0)
    for row in range(ROWS_HERE):
        angles = f32(draft + lengths[row]) * frequencies[...]
        place = pl.ds(row * DRAFT, DRAFT)
        cosines[place] = jnp.cos(angles)
        sines[place] = jnp.sin(angles) * sign

    barrier = pltpu.get_barrier_semaphore()
    for peer in neighbours:
        pl.semaphore_signal(barrier, inc=1, device_id=peer, device_id_type=pl.DeviceIdType.MESH)
    pl.semaphore_wait(barrier, len(neighbours))

    started = []

    def remote(src, dst, row, c, peer):
        return pltpu.make_async_remote_copy(
            src_ref=src,
            dst_ref=dst,
            send_sem=send_sem.at[row, c],
            recv_sem=recv_sem.at[row, c],
            device_id=peer,
            device_id_type=pl.DeviceIdType.MESH,
        )

    def send(src, dst, row, c, peer):
        copy = remote(src, dst, row, c, peer)
        copy.start()
        started.append(copy)

    def arrived(dst, row, c):
        remote(dst, dst, row, c, core_peer).wait_recv()

    def scatter_start(base, c, shard, land, index, plus, minus):
        far = mod4(index + 2)
        send(shard(far, 1), land(0), base, c, plus)
        send(shard(far, 0), land(1), base + 1, c, minus)
        send(shard(mod4(index + 1), 0), land(2), base + 2, c, plus)
        send(shard(mod4(index + 3), 1), land(3), base + 3, c, minus)

    def scatter_mid(base, c, shard, land, index, plus, minus):
        for slot, step, half, peer in ((0, 1, 1, plus), (1, 3, 0, minus)):
            target = mod4(index + step)
            arrived(land(slot), base + slot, c)
            piece = shard(target, half)
            piece[...] = (f32(piece[...]) + f32(land(slot)[...])).astype(piece.dtype)
            send(piece, land(4 + slot), base + 4 + slot, c, peer)

    def to_ring(base, c, part, land, index, peers):
        for slot in (1, 0, 2):
            send(part(slot + 1), land(slot), base + slot, c, peers[slot])

    def scatter_end(base, c, shard, land, index):
        halves = []
        for half, direct, chained in ((0, 2, 5), (1, 3, 4)):
            arrived(land(direct), base + direct, c)
            arrived(land(chained), base + chained, c)
            halves.append(
                f32(shard(index, half)[...]) + f32(land(direct)[...]) + f32(land(chained)[...])
            )
        return halves

    def gather_start(base, c, part, index, plus, minus):
        own = part(index, None)
        send(own, own, base, c, plus)
        send(own, own, base + 1, c, minus)

    def gather_mid(base, c, part, index, plus, minus):
        for slot, step, half, peer in ((0, 3, 0, plus), (1, 1, 1, minus)):
            source = mod4(index + step)
            arrived(part(source, None), base + slot, c)
            piece = part(source, half)
            send(piece, piece, base + 2 + slot, c, peer)

    def gather_end(base, c, part, index):
        far = mod4(index + 2)
        arrived(part(far, 0), base + 2, c)
        arrived(part(far, 1), base + 3, c)

    def project(c):
        states_load(c).wait()
        wide = f32(xs[c]).reshape(M, FEATS)
        squares = jnp.sum(wide * wide, axis=1, keepdims=True)
        scaled[...] = (wide * gain[...]).astype(jnp.bfloat16)
        if c == 0:
            wq_load.wait()
            wkv_load.wait()

        def put(block, start):
            for b in range(NB):
                ybuf[c, b % 2, b // 2, :, start] = block[b * T : (b + 1) * T]

        put(jnp.broadcast_to(squares, (M, HD)), pl.ds(QW + HD, HD))
        put(
            jnp.dot(scaled[...], wkv_v[...], preferred_element_type=jnp.float32), pl.ds(QW, HD)
        )

        put(jnp.dot(scaled[...], wq_v[...], preferred_element_type=jnp.float32), pl.ds(0, QW))
        send(ybuf.at[c, 1 - core], crecv.at[c], CORE, c, core_peer)

    def z_shard(c):
        return lambda t, h: ybuf.at[c, core, t, pl.ds(h * (T // 2), T // 2), :]

    def z_land(c):
        return lambda slot: zrecv.at[c, slot]

    def pair_cores(c):
        arrived(crecv.at[c], CORE, c)
        ybuf[c, core] = ybuf[c, core] + crecv[c]
        scatter_start(ZRS, c, z_shard(c), z_land(c), z, z_plus, z_minus)

    def project_mid(c):
        scatter_mid(ZRS, c, z_shard(c), z_land(c), z, z_plus, z_minus)

    def project_end(c):
        total = jnp.concatenate(scatter_end(ZRS, c, z_shard(c), z_land(c), z), axis=0)
        inverse = lax.rsqrt(total[:, QW + HD :] / D + 1e-05)
        cosine = cosines[c * T : (c + 1) * T]
        sine = sines[c * T : (c + 1) * T]
        half = HD // 2
        for h in range(OWN):
            cols = slice(h * HD, (h + 1) * HD)
            raw = total[:, cols] * qscale[:, cols] * inverse
            turned = jnp.concatenate([raw[:, half:], raw[:, :half]], axis=1)
            query = (raw * cosine + turned * sine).astype(jnp.bfloat16)
            for r in range(CHUNK_ROWS):
                qbuf[c, parity, r, pl.ds(h * DRAFT, DRAFT), :] = query[
                    r * DRAFT : (r + 1) * DRAFT
                ]
        raw = total[:, QW : QW + HD] * kvscale[...] * inverse
        turned = jnp.concatenate([raw[:, half:], raw[:, :half]], axis=1)
        rotated = raw * cosine + turned * sine
        kvbuf[c, parity] = jnp.where(parity == 0, rotated, raw).astype(jnp.bfloat16)
        send(qbuf.at[c, parity], qbuf.at[c, parity], SWAP, c, pair_peer)
        send(kvbuf.at[c, parity], kvbuf.at[c, parity], SWAP + 1, c, pair_peer)

    def attend(c):
        if c == 0:
            kpad[...] = jnp.zeros_like(kpad)
            vpad[...] = jnp.zeros_like(vpad)
            k_load.wait()
            v_load.wait()
        arrived(qbuf.at[c, 1 - parity], SWAP, c)
        arrived(kvbuf.at[c, 1 - parity], SWAP + 1, c)
        place = lax.broadcasted_iota(jnp.int32, (1, SPAN), 1) + parity * SPAN
        token = lax.rem(lax.broadcasted_iota(jnp.int32, (2 * OWN * DRAFT, HD), 0), DRAFT)
        other = lax.broadcasted_iota(jnp.int32, (2 * OWN * DRAFT, HD), 1)
        drafted = (other <= token) & (parity == 0)
        lane = lax.broadcasted_iota(jnp.int32, (QW // OWN, HD), 1)
        for r in range(CHUNK_ROWS):
            row = c * CHUNK_ROWS + r
            kpad[r, 0:DRAFT] = kvbuf[c, 0, r * DRAFT : (r + 1) * DRAFT]
            vpad[r, 0:DRAFT] = kvbuf[c, 1, r * DRAFT : (r + 1) * DRAFT]
            query = jnp.concatenate([qbuf[c, 0, r], qbuf[c, 1, r]], axis=0)
            across = (((1,), (1,)), ((), ()))
            bias = jnp.where(place < lengths[row], 0.0, LOWEST)
            tiles = [slice(i * TILE, (i + 1) * TILE) for i in range(SPAN // TILE)]
            fresh = lax.dot_general(
                query, kpad[r], across, preferred_element_type=jnp.float32
            )
            fresh = jnp.where(drafted, fresh * LOG_SCALE, LOWEST)
            top = jnp.max(fresh, axis=1, keepdims=True)
            scores = []
            for tile in tiles:
                part = lax.dot_general(
                    query, k_v[row, tile], across, preferred_element_type=jnp.float32
                )
                scores.append(part * LOG_SCALE + bias[:, tile])
                top = jnp.maximum(top, jnp.max(scores[-1], axis=1, keepdims=True))
            weights = jnp.exp2(fresh - top)
            totals = jnp.sum(weights, axis=1, keepdims=True)
            weighted = jnp.dot(
                weights.astype(jnp.bfloat16), vpad[r], preferred_element_type=jnp.float32
            )
            for tile, part in zip(tiles, scores):
                weights = jnp.exp2(part - top)
                totals = totals + jnp.sum(weights, axis=1, keepdims=True)
                weighted = weighted + jnp.dot(
                    weights.astype(jnp.bfloat16), v_v[row, tile], preferred_element_type=jnp.float32
                )
            for p in range(2):
                mine = slice(p * QW // OWN, (p + 1) * QW // OWN)
                both = jnp.where(lane < HD // 2, top[mine], totals[mine]).T
                obuf[c, p, r, 0:HD] = weighted[mine]
                obuf[c, p, r, HD : HD + 8] = both[0:8]
                obuf[c, p, r, HD + 8 : HD + 16] = both[HD // 2 : HD // 2 + 8]
            send(obuf.at[c, 1 - parity, r], orecv.at[c, r], FAR + r, c, pair_peer)

    def to_core(c, slot, t):
        block = gat.at[c, 2 * t + core]
        send(block, block, CAG + slot, c, core_peer)

    def combine(c):
        for r in range(CHUNK_ROWS):
            arrived(orecv.at[c, r], FAR + r, c)
            near_top = obuf[c, parity, r, HD : HD + 8]
            near_total = obuf[c, parity, r, HD + 8 : HD + 16]
            far_top = orecv[c, r, HD : HD + 8]
            far_total = orecv[c, r, HD + 8 : HD + 16]
            joint = jnp.maximum(near_top, far_top)
            near_factor = jnp.exp2(near_top - joint)
            far_factor = jnp.exp2(far_top - joint)
            share = 1.0 / (near_total * near_factor + far_total * far_factor)

            def spread(factor):
                return jnp.broadcast_to((factor * share)[0:1], (HD, HD)).T

            heads = (
                obuf[c, parity, r, 0:HD] * spread(near_factor)
                + orecv[c, r, 0:HD] * spread(far_factor)
            ).astype(jnp.bfloat16)
            for h in range(OWN):
                gat[c, din, r * DRAFT : (r + 1) * DRAFT, h * HD : (h + 1) * HD] = heads[
                    h * DRAFT : (h + 1) * DRAFT
                ]
        own = gat.at[c, din]
        to_ring(ZAG, c, lambda step: own, lambda slot: own, z, z_ring)
        to_core(c, 3, z)

    def gather_heads(c):
        for slot in (0, 2, 1):
            t = mod4(z + 3 - slot)
            arrived(gat.at[c, 2 * t + core], ZAG + slot, c)
            to_core(c, slot, t)

    first = ((x, x_plus, x_minus), (y, y_plus, y_minus))
    second = ((y, y_ring), (x, x_ring))

    def columns(side, t):
        return pl.ds(pl.multiple_of((4 * side + t) * WIDTH, WIDTH), WIDTH)

    def rows(c):
        return pl.ds(c * T, T)

    def shard1(c, side):
        return lambda t, h: pbuf.at[c, pl.ds(h * 4, 4), :, columns(side, t)]

    def land1(c, side):
        return lambda slot: r1[c][side].at[slot]

    def part2(c, side, t):
        return out.at[pl.ds(2 * t, 2), rows(c), columns(side, first[side][0])]

    def part1(c, side):
        def part(t, half):
            if half is None:
                return out.at[:, rows(c), columns(side, t)]
            return out.at[pl.ds(half * 4, 4), rows(c), columns(side, t)]

        return part

    def output(c):
        if c == 0:
            wo_load.wait()
        for slot in (3, 0, 2, 1):
            t = mod4(z + 3 - slot)
            arrived(gat.at[c, 2 * t + 1 - core], CAG + slot, c)

        heads = gat[c].reshape(M, QW)
        for side in range(2):
            width = OUTS // 2
            cols = slice(side * width, (side + 1) * width)
            block = jnp.dot(heads, wo_v[:, cols], preferred_element_type=jnp.float32)
            pbuf[c, :, :, cols] = block.astype(jnp.bfloat16).reshape(NB, T, width)
            scatter_start(RS1 + 6 * side, c, shard1(c, side), land1(c, side), *first[side])

    def sum_mid(c):
        for side in range(2):
            scatter_mid(RS1 + 6 * side, c, shard1(c, side), land1(c, side), *first[side])

    def sum_end(c):
        for side in range(2):
            halves = scatter_end(
                RS1 + 6 * side, c, shard1(c, side), land1(c, side), first[side][0]
            )
            for h in range(2):
                gf[c][side][h * 4 : (h + 1) * 4] = halves[h]
                gb[c][side][h * 4 : (h + 1) * 4] = halves[h].astype(jnp.bfloat16)
            index, ring = second[side]
            to_ring(
                RS2 + 3 * side,
                c,
                lambda step: gb[c][side].at[pl.ds(2 * mod4(index + step), 2)],
                lambda slot: r2[c][side].at[slot],
                index,
                ring,
            )

    def cross_end(c):
        for side in range(2):
            index, ring = second[side]
            total = gf[c][side][pl.ds(2 * index, 2)]
            for slot in range(3):
                arrived(r2[c][side].at[slot], RS2 + 3 * side + slot, c)
                total = total + f32(r2[c][side][slot])
            cols = columns(side, first[side][0])
            part2(c, side, index)[...] = (total * oscale[:, cols]).astype(jnp.bfloat16)
            own = part2(c, side, index)
            to_ring(AG2 + 3 * side, c, lambda step: own, lambda slot: own, index, ring)

    def spread_end(c):
        for side in range(2):
            index, _ = second[side]
            for slot in range(3):
                arrived(part2(c, side, mod4(index + 3 - slot)), AG2 + 3 * side + slot, c)
            gather_start(AG1 + 4 * side, c, part1(c, side), *first[side])

    def last_mid(c):
        for side in range(2):
            gather_mid(AG1 + 4 * side, c, part1(c, side), *first[side])

    def last_end(c):
        for side in range(2):
            gather_end(AG1 + 4 * side, c, part1(c, side), first[side][0])

    stages = (
        project,
        pair_cores,
        project_mid,
        project_end,
        attend,
        combine,
        gather_heads,
        output,
        sum_mid,
        sum_end,
        cross_end,
        spread_end,
        last_mid,
        last_end,
    )
    for c, i in ORDER:
        stages[i](c)

    for copy in started:
        copy.wait_send()


def shards(
    states,
    lengths,
    norm_gain,
    query_weight,
    keyval_weight,
    output_weight,
    query_scale,
    keyval_scale,
    output_scale,
    key_cache,
    value_cache,
):
    table = rotary_table(HD)
    frequencies = jnp.concatenate([table, table])[None, :]
    bf16 = jnp.bfloat16
    vmem = pl.BlockSpec(memory_space=pltpu.VMEM)
    smem = pl.BlockSpec(memory_space=pltpu.SMEM)
    hbm = pl.BlockSpec(memory_space=pl.ANY)
    result = pl.pallas_call(
        kernel,
        out_shape=pltpu.VMEM((NB, ROWS_HERE * DRAFT, OUTS), bf16),
        in_specs=[smem] + [vmem] * 5 + [hbm] * 6,
        out_specs=vmem,
        scratch_shapes=[
            pltpu.VMEM((ROWS_HERE * DRAFT, HD), jnp.float32),
            pltpu.VMEM((ROWS_HERE * DRAFT, HD), jnp.float32),
            pltpu.VMEM((NC, NB, T, FEATS), bf16),
            pltpu.VMEM((FEATS, QW), bf16),
            pltpu.VMEM((FEATS, HD), bf16),
            pltpu.VMEM((QW, OUTS), bf16),
            pltpu.VMEM((ROWS_HERE, SPAN, HD), bf16),
            pltpu.VMEM((ROWS_HERE, SPAN, HD), bf16),
            pltpu.VMEM((M, FEATS), bf16),
            pltpu.VMEM((NC, 2, 4, T, WIDE), jnp.float32),
            pltpu.VMEM((NC, 4, T, WIDE), jnp.float32),
            pltpu.VMEM((NC, 6, T // 2, WIDE), jnp.float32),
            pltpu.VMEM((NC, 2, CHUNK_ROWS, OWN * DRAFT, HD), bf16),
            pltpu.VMEM((NC, 2, T, HD), bf16),
            pltpu.VMEM((CHUNK_ROWS, HD, HD), bf16),
            pltpu.VMEM((CHUNK_ROWS, HD, HD), bf16),
            pltpu.VMEM((NC, 2, CHUNK_ROWS, HD + 16, HD), jnp.float32),
            pltpu.VMEM((NC, CHUNK_ROWS, HD + 16, HD), jnp.float32),
            pltpu.VMEM((NC, NB, T, QW), bf16),
            pltpu.VMEM((NC, NB, T, OUTS), bf16),
            pltpu.SemaphoreType.DMA((NC + 5,)),
            pltpu.SemaphoreType.DMA((NSEM, NC)),
            pltpu.SemaphoreType.DMA((NSEM, NC)),
            *(
                shape
                for c in range(NC)
                for _ in range(2)
                for shape in (
                    pltpu.VMEM((6, 4, T, WIDTH), bf16),
                    pltpu.VMEM((NB, T, WIDTH), jnp.float32),
                    pltpu.VMEM((NB, T, WIDTH), bf16),
                    pltpu.VMEM((3, 2, T, WIDTH), bf16),
                )
            ),
        ],
        compiler_params=pltpu.CompilerParams(
            collective_id=0, has_side_effects=True, vmem_limit_bytes=LIMIT * 2**20
        ),
        cost_estimate=pl.CostEstimate(
            flops=12 * 10**9, bytes_accessed=25 * 2**20, transcendentals=2**22
        ),
    )(
        lengths,
        frequencies,
        norm_gain[None, :],
        query_scale[None, :],
        keyval_scale[None, :],
        output_scale[None, :],
        states.reshape(NB, ROWS_HERE * DRAFT, FEATS),
        query_weight,
        keyval_weight,
        output_weight,
        key_cache,
        value_cache,
    )
    return result.reshape(NB * ROWS_HERE * DRAFT, OUTS)


def solution(mesh):
    placed = (
        P(None, "din"),
        P("din"),
        P("din"),
        P("din", "dout"),
        P("din", "dout"),
        P("dout", "din"),
        P("dout"),
        P("dout"),
        P("din"),
        P("din", "dout", None),
        P("din", "dout", None),
    )
    return jax.shard_map(
        shards, mesh=mesh, in_specs=placed, out_specs=P(None, "din"), check_vma=False
    )
```

```python
import functools
import math

import jax
import jax.numpy as jnp
from jax import lax
from jax.experimental import pallas as pl
from jax.experimental.pallas import tpu as pltpu
from jax.sharding import PartitionSpec as P

D = 16384
HQ = 128
KVH = 8
HD = 128
DRAFT = 16
ROWS_HERE = 8
OWN = 8
QW = OWN * HD
WIDE = QW + 2 * HD
SPAN = 2048
TILE = 512
FEATS = 2048
OUTS = 2048

CHUNK_ROWS = 1
NC = ROWS_HERE // CHUNK_ROWS
T = CHUNK_ROWS * DRAFT
NB = 8
M = NB * T
LOG_SCALE = math.log2(math.e) / math.sqrt(HD)
LOWEST = -1e30
LIMIT = 56

WIDTH = OUTS // 8

CORE = 0
ZRS = 1
SWAP = 3
FAR = 5
TOPS = FAR + CHUNK_ROWS
ZAG = TOPS + CHUNK_ROWS
CAG = ZAG + 3
RS1 = CAG + 1
RS2 = RS1 + 4
AG2 = RS2 + 2
AG1 = AG2 + 2
ARRIVALS = AG1 + 4
CORE_OUT, ZRS_OUT, SWAP_OUT, FAR_OUT, ZAG_OUT, CAG_OUT = 0, 1, 2, 4, 5, 6
RS1_OUT, RS2_OUT, AG2_OUT, AG1_OUT, TOPS_OUT = 7, 9, 11, 13, 15
DEPARTURES = 16

ORDER = (
    (0, 0), (1, 0), (0, 1), (4, 0), (1, 1), (4, 1), (0, 2), (5, 0), (3, 0), (1, 2),
    (6, 0), (3, 1), (2, 0), (6, 1), (2, 1), (1, 3), (3, 2), (0, 3), (7, 0), (5, 1),
    (2, 2), (4, 2), (0, 4), (1, 4), (3, 3), (7, 1), (5, 2), (2, 3), (6, 2), (4, 3),
    (0, 5), (7, 2), (3, 4), (5, 3), (1, 5), (2, 4), (6, 3), (0, 6), (4, 4), (7, 3),
    (3, 5), (0, 7), (1, 6), (2, 5), (5, 4), (1, 7), (6, 4), (4, 5), (3, 6), (7, 4),
    (0, 8), (2, 6), (1, 8), (2, 7), (3, 7), (7, 5), (5, 5), (6, 5), (0, 9), (4, 6),
    (1, 9), (2, 8), (4, 7), (3, 8), (7, 6), (0, 10), (7, 7), (5, 6), (1, 10), (4, 8),
    (6, 6), (5, 7), (6, 7), (7, 8), (3, 9), (4, 9), (1, 11), (5, 8), (7, 9), (2, 9),
    (6, 8), (0, 11), (4, 10), (3, 10), (5, 9), (6, 9), (2, 10), (1, 12), (7, 10), (0, 12),
    (5, 10), (4, 11), (6, 10), (3, 11), (5, 11), (2, 11), (7, 11), (6, 11), (1, 13), (4, 12),
    (2, 12), (3, 12), (5, 12), (7, 12), (6, 12), (4, 13), (2, 13), (0, 13), (7, 13), (5, 13),
    (3, 13), (6, 13),
)


def rotary_table(head_size):
    entries = []
    for index in range(head_size // 2):
        inverse = 1.0 / 500000.0 ** (2.0 * index / head_size)
        wavelength = 2.0 * math.pi / inverse
        smooth = min(max((8192.0 / wavelength - 1.0) / 3.0, 0.0), 1.0)
        entries.append((1.0 - smooth) * inverse / 8.0 + smooth * inverse)
    return jnp.asarray(entries, dtype=jnp.float32)


def mod4(v):
    return lax.rem(v, 4)


def f32(v):
    return v.astype(jnp.float32)


def kernel(
    lengths, frequencies, gain, qscale, kvscale, oscale,
    states, wq, wkv, wo, keys, values,
    out,
    cosines, sines,
    xs, wq_v, wkv_v, wo_v, k_v, v_v, scaled,
    ybuf, crecv, zrecv, qbuf, kvbuf, kpad, vpad, obuf, osend, orecv, tops, trecv, gat,
    pbuf,
    load_sem, send_sem, recv_sem,
    *sides,
):
    r1, gf, gb, r2 = (
        [[sides[4 * (2 * c + side) + kind] for side in range(2)] for c in range(NC)]
        for kind in range(4)
    )
    din = lax.axis_index("din")
    dout = lax.axis_index("dout")
    core = lax.rem(din, 2)
    z = lax.div(din, 2)
    x = lax.rem(dout, 4)
    y = lax.div(dout, 4)
    parity = lax.rem(x, 2)
    core_peer = (din + 1 - 2 * core, dout)
    pair_peer = (din, dout + 1 - 2 * parity)
    z_plus = (lax.rem(din + 2, 8), dout)
    z_minus = (lax.rem(din + 6, 8), dout)
    x_plus = (din, 4 * y + mod4(x + 1))
    x_minus = (din, 4 * y + mod4(x + 3))
    y_plus = (din, lax.rem(dout + 4, 16))
    y_minus = (din, lax.rem(dout + 12, 16))
    z_ring = (z_plus, (lax.rem(din + 4, 8), dout), z_minus)
    x_ring = (x_plus, (din, 4 * y + mod4(x + 2)), x_minus)
    y_ring = (y_plus, (din, lax.rem(dout + 8, 16)), y_minus)
    neighbours = (core_peer, *z_ring, *x_ring, *y_ring)

    def load(src, dst, index):
        return pltpu.make_async_copy(src, dst, load_sem.at[index])

    def states_load(c):
        return load(states.at[:, pl.ds(c * T, T), :], xs.at[c], c)

    wq_load = load(wq, wq_v, NC)
    wkv_load = load(wkv, wkv_v, NC + 1)
    wo_load = load(wo, wo_v, NC + 2)
    k_load = load(keys, k_v, NC + 3)
    v_load = load(values, v_v, NC + 4)
    states_load(0).start()
    wq_load.start()
    wkv_load.start()
    for c in range(1, NC):
        states_load(c).start()
    k_load.start()
    v_load.start()
    wo_load.start()

    barrier = pltpu.get_barrier_semaphore()
    for peer in neighbours:
        pl.semaphore_signal(barrier, inc=1, device_id=peer, device_id_type=pl.DeviceIdType.MESH)
    draft = lax.broadcasted_iota(jnp.int32, (DRAFT, HD), 0)
    sign = jnp.where(lax.broadcasted_iota(jnp.int32, (DRAFT, HD), 1) < HD // 2, -1.0, 1.0)
    for row in range(ROWS_HERE):
        angles = f32(draft + lengths[row]) * frequencies[...]
        place = pl.ds(row * DRAFT, DRAFT)
        cosines[place] = jnp.cos(angles)
        sines[place] = jnp.sin(angles) * sign
    pl.semaphore_wait(barrier, len(neighbours))

    def remote(src, dst, out_row, row, c, peer):
        return pltpu.make_async_remote_copy(
            src_ref=src,
            dst_ref=dst,
            send_sem=send_sem.at[out_row, c],
            recv_sem=recv_sem.at[row, c],
            device_id=peer,
            device_id_type=pl.DeviceIdType.MESH,
        )

    def send(src, dst, out_row, row, c, peer):
        remote(src, dst, out_row, row, c, peer).start()

    def arrived(like, row, c):
        remote(like, like, 0, row, c, core_peer).wait_recv()

    def departed(like, out_row, c):
        remote(like, like, out_row, 0, c, core_peer).wait_send()

    def scatter_start(out_row, row, c, shard, land, index, plus, minus):
        far = mod4(index + 2)
        send(shard(far, 1), land.at[0], out_row, row, c, plus)
        send(shard(far, 0), land.at[1], out_row, row, c, minus)
        send(shard(mod4(index + 1), 0), land.at[2], out_row, row + 1, c, plus)
        send(shard(mod4(index + 3), 1), land.at[3], out_row, row + 1, c, minus)

    def scatter_mid(out_row, row, c, shard, land, index, plus, minus):
        arrived(land.at[pl.ds(0, 2)], row, c)
        for slot, step, half, peer in ((0, 1, 1, plus), (1, 3, 0, minus)):
            piece = shard(mod4(index + step), half)
            piece[...] = (f32(piece[...]) + f32(land[slot])).astype(piece.dtype)
            send(piece, land.at[4 + slot], out_row, row + 1, c, peer)

    def to_ring(out_row, rows, c, part, land, index, peers):
        for slot in (1, 0, 2):
            send(part(slot + 1), land(slot), out_row, rows[slot], c, peers[slot])

    def scatter_end(row, c, shard, land, index):
        arrived(land.at[pl.ds(2, 4)], row + 1, c)
        return [
            f32(shard(index, half)[...]) + f32(land[direct]) + f32(land[chained])
            for half, direct, chained in ((0, 2, 5), (1, 3, 4))
        ]

    def gather_start(out_row, row, c, part, index, plus, minus):
        own = part(index, None)
        send(own, own, out_row, row, c, plus)
        send(own, own, out_row, row, c, minus)

    def gather_mid(out_row, row, c, part, like, index, plus, minus):
        arrived(like.at[pl.ds(0, 4)], row, c)
        for step, half, peer in ((3, 0, plus), (1, 1, minus)):
            piece = part(mod4(index + step), half)
            send(piece, piece, out_row, row + 1, c, peer)

    def gather_end(row, c, like):
        arrived(like.at[pl.ds(0, 2)], row + 1, c)

    def project(c):
        states_load(c).wait()
        wide = f32(xs[c]).reshape(M, FEATS)
        squares = jnp.sum(wide * wide, axis=1, keepdims=True)
        scaled[...] = (wide * gain[...]).astype(jnp.bfloat16)
        if c == 0:
            wq_load.wait()
            wkv_load.wait()

        def put(block, start):
            for b in range(NB):
                ybuf[c, b % 2, b // 2, :, start] = block[b * T : (b + 1) * T]

        put(jnp.broadcast_to(squares, (M, HD)), pl.ds(QW + HD, HD))
        put(
            jnp.dot(scaled[...], wkv_v[...], preferred_element_type=jnp.float32), pl.ds(QW, HD)
        )

        put(jnp.dot(scaled[...], wq_v[...], preferred_element_type=jnp.float32), pl.ds(0, QW))
        send(ybuf.at[c, 1 - core], crecv.at[c], CORE_OUT, CORE, c, core_peer)

    def z_shard(c):
        return lambda t, h: ybuf.at[c, core, t, pl.ds(h * (T // 2), T // 2), :]

    def pair_cores(c):
        arrived(crecv.at[c], CORE, c)
        ybuf[c, core] = ybuf[c, core] + crecv[c]
        scatter_start(ZRS_OUT, ZRS, c, z_shard(c), zrecv.at[c], z, z_plus, z_minus)

    def project_mid(c):
        scatter_mid(ZRS_OUT, ZRS, c, z_shard(c), zrecv.at[c], z, z_plus, z_minus)

    def project_end(c):
        total = jnp.concatenate(scatter_end(ZRS, c, z_shard(c), zrecv.at[c], z), axis=0)
        inverse = lax.rsqrt(total[:, QW + HD :] / D + 1e-05)
        cosine = cosines[c * T : (c + 1) * T]
        sine = sines[c * T : (c + 1) * T]
        half = HD // 2
        for h in range(OWN):
            cols = slice(h * HD, (h + 1) * HD)
            raw = total[:, cols] * qscale[:, cols] * inverse
            turned = jnp.concatenate([raw[:, half:], raw[:, :half]], axis=1)
            query = (raw * cosine + turned * sine).astype(jnp.bfloat16)
            for r in range(CHUNK_ROWS):
                qbuf[c, parity, r, pl.ds(h * DRAFT, DRAFT), :] = query[
                    r * DRAFT : (r + 1) * DRAFT
                ]
        raw = total[:, QW : QW + HD] * kvscale[...] * inverse
        turned = jnp.concatenate([raw[:, half:], raw[:, :half]], axis=1)
        rotated = raw * cosine + turned * sine
        kvbuf[c, parity] = jnp.where(parity == 0, rotated, raw).astype(jnp.bfloat16)
        send(qbuf.at[c, parity], qbuf.at[c, parity], SWAP_OUT, SWAP, c, pair_peer)
        send(kvbuf.at[c, parity], kvbuf.at[c, parity], SWAP_OUT + 1, SWAP + 1, c, pair_peer)

    def attend(c):
        if c == 0:
            kpad[...] = jnp.zeros_like(kpad)
            vpad[...] = jnp.zeros_like(vpad)
            k_load.wait()
            v_load.wait()
        arrived(qbuf.at[c, 1 - parity], SWAP, c)
        arrived(kvbuf.at[c, 1 - parity], SWAP + 1, c)
        place = lax.broadcasted_iota(jnp.int32, (1, SPAN), 1) + parity * SPAN
        token = lax.rem(lax.broadcasted_iota(jnp.int32, (2 * OWN * DRAFT, HD), 0), DRAFT)
        other = lax.broadcasted_iota(jnp.int32, (2 * OWN * DRAFT, HD), 1)
        drafted = (other <= token) & (parity == 0)
        lane = lax.broadcasted_iota(jnp.int32, (QW // OWN, HD), 1)
        for r in range(CHUNK_ROWS):
            row = c * CHUNK_ROWS + r
            kpad[r, 0:DRAFT] = kvbuf[c, 0, r * DRAFT : (r + 1) * DRAFT]
            vpad[r, 0:DRAFT] = kvbuf[c, 1, r * DRAFT : (r + 1) * DRAFT]
            query = jnp.concatenate([qbuf[c, 0, r], qbuf[c, 1, r]], axis=0)
            across = (((1,), (1,)), ((), ()))
            bias = jnp.where(place < lengths[row], 0.0, LOWEST)
            tiles = [slice(i * TILE, (i + 1) * TILE) for i in range(SPAN // TILE)]
            fresh = lax.dot_general(
                query, kpad[r], across, preferred_element_type=jnp.float32
            )
            fresh = jnp.where(drafted, fresh * LOG_SCALE, LOWEST)
            top = jnp.max(fresh, axis=1, keepdims=True)
            scores = []
            for tile in tiles:
                part = lax.dot_general(
                    query, k_v[row, tile], across, preferred_element_type=jnp.float32
                )
                scores.append(part * LOG_SCALE + bias[:, tile])
                top = jnp.maximum(top, jnp.max(scores[-1], axis=1, keepdims=True))
            weights = jnp.exp2(fresh - top)
            totals = jnp.sum(weights, axis=1, keepdims=True)
            weighted = jnp.dot(
                weights.astype(jnp.bfloat16), vpad[r], preferred_element_type=jnp.float32
            )
            for tile, part in zip(tiles, scores):
                weights = jnp.exp2(part - top)
                totals = totals + jnp.sum(weights, axis=1, keepdims=True)
                weighted = weighted + jnp.dot(
                    weights.astype(jnp.bfloat16), v_v[row, tile], preferred_element_type=jnp.float32
                )
            for p in range(2):
                mine = slice(p * QW // OWN, (p + 1) * QW // OWN)
                both = jnp.where(lane < HD // 2, top[mine], totals[mine]).T
                obuf[c, p, r] = weighted[mine]
                osend[c, p, r] = weighted[mine].astype(jnp.bfloat16)
                tops[c, p, r, 0:4] = both[0:4]
                tops[c, p, r, 4:8] = both[HD // 2 : HD // 2 + 4]
            far = 1 - parity
            send(tops.at[c, far, r], trecv.at[c, r], TOPS_OUT, TOPS + r, c, pair_peer)
            send(osend.at[c, far, r], orecv.at[c, r], FAR_OUT, FAR + r, c, pair_peer)

    def to_core(c, t):
        block = gat.at[c, 2 * t + core]
        send(block, block, CAG_OUT, CAG, c, core_peer)

    def combine(c):
        for r in range(CHUNK_ROWS):
            arrived(trecv.at[c, r], TOPS + r, c)
            arrived(orecv.at[c, r], FAR + r, c)
            near_top, near_total = tops[c, parity, r, 0:4], tops[c, parity, r, 4:8]
            far_top, far_total = trecv[c, r, 0:4], trecv[c, r, 4:8]
            joint = jnp.maximum(near_top, far_top)
            near_factor = jnp.exp2(near_top - joint)
            far_factor = jnp.exp2(far_top - joint)
            share = 1.0 / (near_total * near_factor + far_total * far_factor)

            def spread(factor):
                return jnp.broadcast_to((factor * share)[0:1], (HD, HD)).T

            heads = (
                obuf[c, parity, r] * spread(near_factor)
                + f32(orecv[c, r]) * spread(far_factor)
            ).astype(jnp.bfloat16)
            for h in range(OWN):
                gat[c, din, r * DRAFT : (r + 1) * DRAFT, h * HD : (h + 1) * HD] = heads[
                    h * DRAFT : (h + 1) * DRAFT
                ]
        own = gat.at[c, din]
        rows = (ZAG, ZAG + 1, ZAG + 2)
        to_ring(ZAG_OUT, rows, c, lambda step: own, lambda slot: own, z, z_ring)
        to_core(c, z)

    def gather_heads(c):
        for slot in (0, 2, 1):
            t = mod4(z + 3 - slot)
            arrived(gat.at[c, 2 * t + core], ZAG + slot, c)
            to_core(c, t)

    first = ((x, x_plus, x_minus), (y, y_plus, y_minus))
    second = ((y, y_ring), (x, x_ring))

    def columns(side, t):
        return pl.ds(pl.multiple_of((4 * side + t) * WIDTH, WIDTH), WIDTH)

    def rows(c):
        return pl.ds(c * T, T)

    def shard1(c, side):
        return lambda t, h: pbuf.at[c, pl.ds(h * 4, 4), :, columns(side, t)]

    def part2(c, side, t):
        return out.at[pl.ds(2 * t, 2), rows(c), columns(side, first[side][0])]

    def part1(c, side):
        def part(t, half):
            if half is None:
                return out.at[:, rows(c), columns(side, t)]
            return out.at[pl.ds(half * 4, 4), rows(c), columns(side, t)]

        return part

    def output(c):
        if c == 0:
            wo_load.wait()
        arrived(gat.at[c, pl.ds(0, 4)], CAG, c)

        heads = gat[c].reshape(M, QW)
        for side in range(2):
            width = OUTS // 2
            cols = slice(side * width, (side + 1) * width)
            block = jnp.dot(heads, wo_v[:, cols], preferred_element_type=jnp.float32)
            pbuf[c, :, :, cols] = block.astype(jnp.bfloat16).reshape(NB, T, width)
            sums = (c, shard1(c, side), r1[c][side], *first[side])
            scatter_start(RS1_OUT + side, RS1 + 2 * side, *sums)

    def sum_mid(c):
        for side in range(2):
            sums = (c, shard1(c, side), r1[c][side], *first[side])
            scatter_mid(RS1_OUT + side, RS1 + 2 * side, *sums)

    def sum_end(c):
        for side in range(2):
            halves = scatter_end(
                RS1 + 2 * side, c, shard1(c, side), r1[c][side], first[side][0]
            )
            for h in range(2):
                gf[c][side][h * 4 : (h + 1) * 4] = halves[h]
                gb[c][side][h * 4 : (h + 1) * 4] = halves[h].astype(jnp.bfloat16)
            index, ring = second[side]
            to_ring(
                RS2_OUT + side,
                (RS2 + side,) * 3,
                c,
                lambda step: gb[c][side].at[pl.ds(2 * mod4(index + step), 2)],
                lambda slot: r2[c][side].at[slot],
                index,
                ring,
            )

    def cross_end(c):
        for side in range(2):
            index, ring = second[side]
            total = gf[c][side][pl.ds(2 * index, 2)]
            arrived(r2[c][side], RS2 + side, c)
            for slot in range(3):
                total = total + f32(r2[c][side][slot])
            cols = columns(side, first[side][0])
            part2(c, side, index)[...] = (total * oscale[:, cols]).astype(jnp.bfloat16)
            own = part2(c, side, index)
            to_ring(
                AG2_OUT + side,
                (AG2 + side,) * 3,
                c,
                lambda step: own,
                lambda slot: own,
                index,
                ring,
            )

    def spread_end(c):
        for side in range(2):
            arrived(r2[c][side], AG2 + side, c)
            gather_start(AG1_OUT + side, AG1 + 2 * side, c, part1(c, side), *first[side])

    def last_mid(c):
        for side in range(2):
            spread = (c, part1(c, side), r1[c][side], *first[side])
            gather_mid(AG1_OUT + side, AG1 + 2 * side, *spread)

    def last_end(c):
        for side in range(2):
            gather_end(AG1 + 2 * side, c, r1[c][side])

    stages = (
        project,
        pair_cores,
        project_mid,
        project_end,
        attend,
        combine,
        gather_heads,
        output,
        sum_mid,
        sum_end,
        cross_end,
        spread_end,
        last_mid,
        last_end,
    )
    for c, i in ORDER:
        stages[i](c)

    for c in range(NC):
        departed(crecv.at[c], CORE_OUT, c)
        departed(zrecv.at[c], ZRS_OUT, c)
        departed(qbuf.at[c, 0], SWAP_OUT, c)
        departed(kvbuf.at[c, 0], SWAP_OUT + 1, c)
        departed(orecv.at[c], FAR_OUT, c)
        departed(trecv.at[c], TOPS_OUT, c)
        departed(gat.at[c, pl.ds(0, 3)], ZAG_OUT, c)
        departed(gat.at[c, pl.ds(0, 4)], CAG_OUT, c)
        for side in range(2):
            departed(r1[c][side], RS1_OUT + side, c)
            departed(r2[c][side], RS2_OUT + side, c)
            departed(r2[c][side], AG2_OUT + side, c)
            departed(r1[c][side], AG1_OUT + side, c)


def shards(
    states,
    lengths,
    norm_gain,
    query_weight,
    keyval_weight,
    output_weight,
    query_scale,
    keyval_scale,
    output_scale,
    key_cache,
    value_cache,
):
    table = rotary_table(HD)
    frequencies = jnp.concatenate([table, table])[None, :]
    bf16 = jnp.bfloat16
    vmem = pl.BlockSpec(memory_space=pltpu.VMEM)
    smem = pl.BlockSpec(memory_space=pltpu.SMEM)
    hbm = pl.BlockSpec(memory_space=pl.ANY)
    result = pl.pallas_call(
        kernel,
        out_shape=pltpu.VMEM((NB, ROWS_HERE * DRAFT, OUTS), bf16),
        in_specs=[smem] + [vmem] * 5 + [hbm] * 6,
        out_specs=vmem,
        scratch_shapes=[
            pltpu.VMEM((ROWS_HERE * DRAFT, HD), jnp.float32),
            pltpu.VMEM((ROWS_HERE * DRAFT, HD), jnp.float32),
            pltpu.VMEM((NC, NB, T, FEATS), bf16),
            pltpu.VMEM((FEATS, QW), bf16),
            pltpu.VMEM((FEATS, HD), bf16),
            pltpu.VMEM((QW, OUTS), bf16),
            pltpu.VMEM((ROWS_HERE, SPAN, HD), bf16),
            pltpu.VMEM((ROWS_HERE, SPAN, HD), bf16),
            pltpu.VMEM((M, FEATS), bf16),
            pltpu.VMEM((NC, 2, 4, T, WIDE), jnp.float32),
            pltpu.VMEM((NC, 4, T, WIDE), jnp.float32),
            pltpu.VMEM((NC, 6, T // 2, WIDE), jnp.float32),
            pltpu.VMEM((NC, 2, CHUNK_ROWS, OWN * DRAFT, HD), bf16),
            pltpu.VMEM((NC, 2, T, HD), bf16),
            pltpu.VMEM((CHUNK_ROWS, HD, HD), bf16),
            pltpu.VMEM((CHUNK_ROWS, HD, HD), bf16),
            pltpu.VMEM((NC, 2, CHUNK_ROWS, HD, HD), jnp.float32),
            pltpu.VMEM((NC, 2, CHUNK_ROWS, HD, HD), bf16),
            pltpu.VMEM((NC, CHUNK_ROWS, HD, HD), bf16),
            pltpu.VMEM((NC, 2, CHUNK_ROWS, 8, HD), jnp.float32),
            pltpu.VMEM((NC, CHUNK_ROWS, 8, HD), jnp.float32),
            pltpu.VMEM((NC, NB, T, QW), bf16),
            pltpu.VMEM((NC, NB, T, OUTS), bf16),
            pltpu.SemaphoreType.DMA((NC + 5,)),
            pltpu.SemaphoreType.DMA((DEPARTURES, NC)),
            pltpu.SemaphoreType.DMA((ARRIVALS, NC)),
            *(
                shape
                for c in range(NC)
                for _ in range(2)
                for shape in (
                    pltpu.VMEM((6, 4, T, WIDTH), bf16),
                    pltpu.VMEM((NB, T, WIDTH), jnp.float32),
                    pltpu.VMEM((NB, T, WIDTH), bf16),
                    pltpu.VMEM((3, 2, T, WIDTH), bf16),
                )
            ),
        ],
        compiler_params=pltpu.CompilerParams(
            collective_id=0, has_side_effects=True, vmem_limit_bytes=LIMIT * 2**20
        ),
        cost_estimate=pl.CostEstimate(
            flops=12 * 10**9, bytes_accessed=25 * 2**20, transcendentals=2**22
        ),
    )(
        lengths,
        frequencies,
        norm_gain[None, :],
        query_scale[None, :],
        keyval_scale[None, :],
        output_scale[None, :],
        states.reshape(NB, ROWS_HERE * DRAFT, FEATS),
        query_weight,
        keyval_weight,
        output_weight,
        key_cache,
        value_cache,
    )
    return result.reshape(NB * ROWS_HERE * DRAFT, OUTS)


def solution(mesh):
    placed = (
        P(None, "din"),
        P("din"),
        P("din"),
        P("din", "dout"),
        P("din", "dout"),
        P("dout", "din"),
        P("dout"),
        P("dout"),
        P("din"),
        P("din", "dout", None),
        P("din", "dout", None),
    )
    return jax.shard_map(
        shards, mesh=mesh, in_specs=placed, out_specs=P(None, "din"), check_vma=False
    )
```

```python
import functools
import math

import jax
import jax.numpy as jnp
from jax import lax
from jax.experimental import pallas as pl
from jax.experimental.pallas import tpu as pltpu
from jax.sharding import PartitionSpec as P

D = 16384
HQ = 128
KVH = 8
HD = 128
DRAFT = 16
ROWS_HERE = 8
OWN = 8
QW = OWN * HD
WIDE = QW + HD
SPAN = 2048
TILE = 512
FEATS = 2048
OUTS = 2048

CHUNK_ROWS = 1
NC = ROWS_HERE // CHUNK_ROWS
T = CHUNK_ROWS * DRAFT
NB = 8
M = NB * T
LOG_SCALE = math.log2(math.e) / math.sqrt(HD)
LOWEST = -1e30
LIMIT = 56

WIDTH = OUTS // 8

CORE = 0
ZRS = 1
SWAP = 3
FAR = 5
TOPS = FAR + CHUNK_ROWS
ZAG = TOPS + CHUNK_ROWS
CAG = ZAG + 3
SQC = CAG + 1
SQZ = SQC + 1
RS1 = SQZ + 1
RS2 = RS1 + 4
AG2 = RS2 + 2
AG1 = AG2 + 2
ARRIVALS = AG1 + 4
CORE_OUT, ZRS_OUT, SWAP_OUT, FAR_OUT, ZAG_OUT, CAG_OUT = 0, 1, 2, 4, 5, 6
RS1_OUT, RS2_OUT, AG2_OUT, AG1_OUT, TOPS_OUT, SQC_OUT, SQZ_OUT = 7, 9, 11, 13, 15, 16, 17
DEPARTURES = 18

ORDER = (
    (0, 0), (1, 0), (0, 1), (3, 0), (1, 1), (2, 0), (7, 0), (3, 1), (4, 0), (0, 2),
    (1, 2), (5, 0), (2, 1), (3, 2), (4, 1), (0, 3), (1, 3), (2, 2), (5, 1), (6, 0),
    (3, 3), (4, 2), (6, 1), (0, 4), (2, 3), (5, 2), (7, 1), (1, 4), (3, 4), (4, 3),
    (6, 2), (0, 5), (5, 3), (2, 4), (7, 2), (1, 5), (3, 5), (6, 3), (4, 4), (0, 6),
    (5, 4), (2, 5), (7, 3), (0, 7), (1, 6), (6, 4), (3, 6), (1, 7), (5, 5), (7, 4),
    (2, 6), (4, 5), (0, 8), (3, 7), (2, 7), (6, 5), (5, 6), (1, 8), (7, 5), (0, 9),
    (4, 6), (5, 7), (2, 8), (4, 7), (6, 6), (7, 6), (0, 10), (3, 8), (7, 7), (6, 7),
    (1, 9), (5, 8), (3, 9), (2, 9), (4, 8), (0, 11), (5, 9), (6, 8), (3, 10), (1, 10),
    (4, 9), (7, 8), (0, 12), (2, 10), (5, 10), (6, 9), (4, 10), (7, 9), (1, 11), (5, 11),
    (4, 11), (7, 10), (6, 10), (0, 13), (2, 11), (3, 11), (5, 12), (6, 11), (7, 11), (2, 12),
    (1, 12), (4, 12), (3, 12), (6, 12), (7, 12), (3, 13), (6, 13), (4, 13), (1, 13), (5, 13),
    (2, 13), (7, 13),
)


def rotary_table(head_size):
    entries = []
    for index in range(head_size // 2):
        inverse = 1.0 / 500000.0 ** (2.0 * index / head_size)
        wavelength = 2.0 * math.pi / inverse
        smooth = min(max((8192.0 / wavelength - 1.0) / 3.0, 0.0), 1.0)
        entries.append((1.0 - smooth) * inverse / 8.0 + smooth * inverse)
    return jnp.asarray(entries, dtype=jnp.float32)


def mod4(v):
    return lax.rem(v, 4)


def f32(v):
    return v.astype(jnp.float32)


def kernel(
    lengths, frequencies, gain, qscale, kvscale, oscale,
    states, wq, wkv, wo, keys, values,
    out,
    cosines, sines,
    xs, wq_v, wkv_v, wo_v, k_v, v_v, scaled,
    ybuf, crecv, zrecv, squares, landed, inverses, qbuf, kvbuf, kpad, vpad, obuf, osend, orecv, tops, trecv, gat,
    pbuf,
    load_sem, send_sem, recv_sem,
    *sides,
):
    r1, gf, gb, r2 = (
        [[sides[4 * (2 * c + side) + kind] for side in range(2)] for c in range(NC)]
        for kind in range(4)
    )
    din = lax.axis_index("din")
    dout = lax.axis_index("dout")
    core = lax.rem(din, 2)
    z = lax.div(din, 2)
    x = lax.rem(dout, 4)
    y = lax.div(dout, 4)
    parity = lax.rem(x, 2)
    core_peer = (din + 1 - 2 * core, dout)
    pair_peer = (din, dout + 1 - 2 * parity)
    z_plus = (lax.rem(din + 2, 8), dout)
    z_minus = (lax.rem(din + 6, 8), dout)
    x_plus = (din, 4 * y + mod4(x + 1))
    x_minus = (din, 4 * y + mod4(x + 3))
    y_plus = (din, lax.rem(dout + 4, 16))
    y_minus = (din, lax.rem(dout + 12, 16))
    z_ring = (z_plus, (lax.rem(din + 4, 8), dout), z_minus)
    x_ring = (x_plus, (din, 4 * y + mod4(x + 2)), x_minus)
    y_ring = (y_plus, (din, lax.rem(dout + 8, 16)), y_minus)
    neighbours = (core_peer, *z_ring, *x_ring, *y_ring)

    def load(src, dst, index):
        return pltpu.make_async_copy(src, dst, load_sem.at[index])

    def states_load(c):
        return load(states.at[:, pl.ds(c * T, T), :], xs.at[c], c)

    wq_load = load(wq, wq_v, NC)
    wkv_load = load(wkv, wkv_v, NC + 1)
    wo_load = load(wo, wo_v, NC + 2)
    k_load = load(keys, k_v, NC + 3)
    v_load = load(values, v_v, NC + 4)
    states_load(0).start()
    wq_load.start()
    wkv_load.start()
    for c in range(1, NC):
        states_load(c).start()
    k_load.start()
    v_load.start()
    wo_load.start()

    barrier = pltpu.get_barrier_semaphore()
    for peer in neighbours:
        pl.semaphore_signal(barrier, inc=1, device_id=peer, device_id_type=pl.DeviceIdType.MESH)
    draft = lax.broadcasted_iota(jnp.int32, (DRAFT, HD), 0)
    sign = jnp.where(lax.broadcasted_iota(jnp.int32, (DRAFT, HD), 1) < HD // 2, -1.0, 1.0)
    for row in range(ROWS_HERE):
        angles = f32(draft + lengths[row]) * frequencies[...]
        place = pl.ds(row * DRAFT, DRAFT)
        cosines[place] = jnp.cos(angles)
        sines[place] = jnp.sin(angles) * sign
    pl.semaphore_wait(barrier, len(neighbours))

    def remote(src, dst, out_row, row, c, peer):
        return pltpu.make_async_remote_copy(
            src_ref=src,
            dst_ref=dst,
            send_sem=send_sem.at[out_row, c],
            recv_sem=recv_sem.at[row, c],
            device_id=peer,
            device_id_type=pl.DeviceIdType.MESH,
        )

    def send(src, dst, out_row, row, c, peer):
        remote(src, dst, out_row, row, c, peer).start()

    def arrived(like, row, c):
        remote(like, like, 0, row, c, core_peer).wait_recv()

    def departed(like, out_row, c):
        remote(like, like, out_row, 0, c, core_peer).wait_send()

    def scatter_start(out_row, row, c, shard, land, index, plus, minus):
        far = mod4(index + 2)
        send(shard(far, 1), land.at[0], out_row, row, c, plus)
        send(shard(far, 0), land.at[1], out_row, row, c, minus)
        send(shard(mod4(index + 1), 0), land.at[2], out_row, row + 1, c, plus)
        send(shard(mod4(index + 3), 1), land.at[3], out_row, row + 1, c, minus)

    def scatter_mid(out_row, row, c, shard, land, index, plus, minus):
        arrived(land.at[pl.ds(0, 2)], row, c)
        for slot, step, half, peer in ((0, 1, 1, plus), (1, 3, 0, minus)):
            piece = shard(mod4(index + step), half)
            piece[...] = (f32(piece[...]) + f32(land[slot])).astype(piece.dtype)
            send(piece, land.at[4 + slot], out_row, row + 1, c, peer)

    def to_ring(out_row, rows, c, part, land, index, peers):
        for slot in (1, 0, 2):
            send(part(slot + 1), land(slot), out_row, rows[slot], c, peers[slot])

    def scatter_end(row, c, shard, land, index):
        arrived(land.at[pl.ds(2, 4)], row + 1, c)
        return [
            f32(shard(index, half)[...]) + f32(land[direct]) + f32(land[chained])
            for half, direct, chained in ((0, 2, 5), (1, 3, 4))
        ]

    def gather_start(out_row, row, c, part, index, plus, minus):
        own = part(index, None)
        send(own, own, out_row, row, c, plus)
        send(own, own, out_row, row, c, minus)

    def gather_mid(out_row, row, c, part, like, index, plus, minus):
        arrived(like.at[pl.ds(0, 4)], row, c)
        for step, half, peer in ((3, 0, plus), (1, 1, minus)):
            piece = part(mod4(index + step), half)
            send(piece, piece, out_row, row + 1, c, peer)

    def gather_end(row, c, like):
        arrived(like.at[pl.ds(0, 2)], row + 1, c)

    def project(c):
        states_load(c).wait()
        wide = f32(xs[c]).reshape(M, FEATS)
        column = jnp.sum(wide * wide, axis=1, keepdims=True)
        squares[c, 0] = jnp.broadcast_to(column, (M, M)).T[0:1]
        send(squares.at[c, 0], landed.at[c, 0], SQC_OUT, SQC, c, core_peer)
        scaled[...] = (wide * gain[...]).astype(jnp.bfloat16)
        if c == 0:
            wq_load.wait()
            wkv_load.wait()

        def put(block, start):
            for b in range(NB):
                ybuf[c, b % 2, b // 2, :, start] = block[b * T : (b + 1) * T]

        put(
            jnp.dot(scaled[...], wkv_v[...], preferred_element_type=jnp.float32), pl.ds(QW, HD)
        )

        put(jnp.dot(scaled[...], wq_v[...], preferred_element_type=jnp.float32), pl.ds(0, QW))
        send(ybuf.at[c, 1 - core], crecv.at[c], CORE_OUT, CORE, c, core_peer)

    def z_shard(c):
        return lambda t, h: ybuf.at[c, core, t, pl.ds(h * (T // 2), T // 2), :]

    def pair_cores(c):
        arrived(crecv.at[c], CORE, c)
        ybuf[c, core] = ybuf[c, core] + crecv[c]
        scatter_start(ZRS_OUT, ZRS, c, z_shard(c), zrecv.at[c], z, z_plus, z_minus)
        arrived(landed.at[c, 0], SQC, c)
        squares[c, 1] = squares[c, 0] + landed[c, 0]
        own = squares.at[c, 1]
        to_ring(
            SQZ_OUT, (SQZ,) * 3, c, lambda step: own, lambda k: landed.at[c, k + 1], z, z_ring
        )

    def project_mid(c):
        scatter_mid(ZRS_OUT, ZRS, c, z_shard(c), zrecv.at[c], z, z_plus, z_minus)

    def project_end(c):
        total = jnp.concatenate(scatter_end(ZRS, c, z_shard(c), zrecv.at[c], z), axis=0)
        arrived(landed.at[c, pl.ds(1, 3)], SQZ, c)
        summed = squares[c, 1] + landed[c, 1] + landed[c, 2] + landed[c, 3]
        row = lax.rsqrt(summed / D + 1e-05)
        inverses[...] = jnp.broadcast_to(row, (M, M)).T
        inverse = inverses[pl.ds(pl.multiple_of(din * T, T), T)]
        cosine = cosines[c * T : (c + 1) * T]
        sine = sines[c * T : (c + 1) * T]
        half = HD // 2
        for h in range(OWN):
            cols = slice(h * HD, (h + 1) * HD)
            raw = total[:, cols] * qscale[:, cols] * inverse
            turned = jnp.concatenate([raw[:, half:], raw[:, :half]], axis=1)
            query = (raw * cosine + turned * sine).astype(jnp.bfloat16)
            for r in range(CHUNK_ROWS):
                qbuf[c, parity, r, pl.ds(h * DRAFT, DRAFT), :] = query[
                    r * DRAFT : (r + 1) * DRAFT
                ]
        raw = total[:, QW : QW + HD] * kvscale[...] * inverse
        turned = jnp.concatenate([raw[:, half:], raw[:, :half]], axis=1)
        rotated = raw * cosine + turned * sine
        kvbuf[c, parity] = jnp.where(parity == 0, rotated, raw).astype(jnp.bfloat16)
        send(qbuf.at[c, parity], qbuf.at[c, parity], SWAP_OUT, SWAP, c, pair_peer)
        send(kvbuf.at[c, parity], kvbuf.at[c, parity], SWAP_OUT + 1, SWAP + 1, c, pair_peer)

    def attend(c):
        if c == 0:
            kpad[...] = jnp.zeros_like(kpad)
            vpad[...] = jnp.zeros_like(vpad)
            k_load.wait()
            v_load.wait()
        arrived(qbuf.at[c, 1 - parity], SWAP, c)
        arrived(kvbuf.at[c, 1 - parity], SWAP + 1, c)
        place = lax.broadcasted_iota(jnp.int32, (1, SPAN), 1) + parity * SPAN
        token = lax.rem(lax.broadcasted_iota(jnp.int32, (2 * OWN * DRAFT, HD), 0), DRAFT)
        other = lax.broadcasted_iota(jnp.int32, (2 * OWN * DRAFT, HD), 1)
        drafted = (other <= token) & (parity == 0)
        lane = lax.broadcasted_iota(jnp.int32, (QW // OWN, HD), 1)
        for r in range(CHUNK_ROWS):
            row = c * CHUNK_ROWS + r
            kpad[r, 0:DRAFT] = kvbuf[c, 0, r * DRAFT : (r + 1) * DRAFT]
            vpad[r, 0:DRAFT] = kvbuf[c, 1, r * DRAFT : (r + 1) * DRAFT]
            query = jnp.concatenate([qbuf[c, 0, r], qbuf[c, 1, r]], axis=0)
            across = (((1,), (1,)), ((), ()))
            bias = jnp.where(place < lengths[row], 0.0, LOWEST)
            tiles = [slice(i * TILE, (i + 1) * TILE) for i in range(SPAN // TILE)]
            fresh = lax.dot_general(
                query, kpad[r], across, preferred_element_type=jnp.float32
            )
            fresh = jnp.where(drafted, fresh * LOG_SCALE, LOWEST)
            top = jnp.max(fresh, axis=1, keepdims=True)
            scores = []
            for tile in tiles:
                part = lax.dot_general(
                    query, k_v[row, tile], across, preferred_element_type=jnp.float32
                )
                scores.append(part * LOG_SCALE + bias[:, tile])
                top = jnp.maximum(top, jnp.max(scores[-1], axis=1, keepdims=True))
            weights = jnp.exp2(fresh - top)
            totals = jnp.sum(weights, axis=1, keepdims=True)
            weighted = jnp.dot(
                weights.astype(jnp.bfloat16), vpad[r], preferred_element_type=jnp.float32
            )
            for tile, part in zip(tiles, scores):
                weights = jnp.exp2(part - top)
                totals = totals + jnp.sum(weights, axis=1, keepdims=True)
                weighted = weighted + jnp.dot(
                    weights.astype(jnp.bfloat16), v_v[row, tile], preferred_element_type=jnp.float32
                )
            for p in range(2):
                mine = slice(p * QW // OWN, (p + 1) * QW // OWN)
                both = jnp.where(lane < HD // 2, top[mine], totals[mine]).T
                obuf[c, p, r] = weighted[mine]
                osend[c, p, r] = weighted[mine].astype(jnp.bfloat16)
                tops[c, p, r, 0:4] = both[0:4]
                tops[c, p, r, 4:8] = both[HD // 2 : HD // 2 + 4]
            far = 1 - parity
            send(tops.at[c, far, r], trecv.at[c, r], TOPS_OUT, TOPS + r, c, pair_peer)
            send(osend.at[c, far, r], orecv.at[c, r], FAR_OUT, FAR + r, c, pair_peer)

    def to_core(c, t):
        block = gat.at[c, 2 * t + core]
        send(block, block, CAG_OUT, CAG, c, core_peer)

    def combine(c):
        for r in range(CHUNK_ROWS):
            arrived(trecv.at[c, r], TOPS + r, c)
            arrived(orecv.at[c, r], FAR + r, c)
            near_top, near_total = tops[c, parity, r, 0:4], tops[c, parity, r, 4:8]
            far_top, far_total = trecv[c, r, 0:4], trecv[c, r, 4:8]
            joint = jnp.maximum(near_top, far_top)
            near_factor = jnp.exp2(near_top - joint)
            far_factor = jnp.exp2(far_top - joint)
            share = 1.0 / (near_total * near_factor + far_total * far_factor)

            def spread(factor):
                return jnp.broadcast_to((factor * share)[0:1], (HD, HD)).T

            heads = (
                obuf[c, parity, r] * spread(near_factor)
                + f32(orecv[c, r]) * spread(far_factor)
            ).astype(jnp.bfloat16)
            for h in range(OWN):
                gat[c, din, r * DRAFT : (r + 1) * DRAFT, h * HD : (h + 1) * HD] = heads[
                    h * DRAFT : (h + 1) * DRAFT
                ]
        own = gat.at[c, din]
        rows = (ZAG, ZAG + 1, ZAG + 2)
        to_ring(ZAG_OUT, rows, c, lambda step: own, lambda slot: own, z, z_ring)
        to_core(c, z)

    def gather_heads(c):
        for slot in (0, 2, 1):
            t = mod4(z + 3 - slot)
            arrived(gat.at[c, 2 * t + core], ZAG + slot, c)
            to_core(c, t)

    first = ((x, x_plus, x_minus), (y, y_plus, y_minus))
    second = ((y, y_ring), (x, x_ring))

    def columns(side, t):
        return pl.ds(pl.multiple_of((4 * side + t) * WIDTH, WIDTH), WIDTH)

    def rows(c):
        return pl.ds(c * T, T)

    def shard1(c, side):
        return lambda t, h: pbuf.at[c, pl.ds(h * 4, 4), :, columns(side, t)]

    def part2(c, side, t):
        return out.at[pl.ds(2 * t, 2), rows(c), columns(side, first[side][0])]

    def part1(c, side):
        def part(t, half):
            if half is None:
                return out.at[:, rows(c), columns(side, t)]
            return out.at[pl.ds(half * 4, 4), rows(c), columns(side, t)]

        return part

    def output(c):
        if c == 0:
            wo_load.wait()
        arrived(gat.at[c, pl.ds(0, 4)], CAG, c)

        heads = gat[c].reshape(M, QW)
        for side in range(2):
            width = OUTS // 2
            cols = slice(side * width, (side + 1) * width)
            block = jnp.dot(heads, wo_v[:, cols], preferred_element_type=jnp.float32)
            pbuf[c, :, :, cols] = block.astype(jnp.bfloat16).reshape(NB, T, width)
            sums = (c, shard1(c, side), r1[c][side], *first[side])
            scatter_start(RS1_OUT + side, RS1 + 2 * side, *sums)

    def sum_mid(c):
        for side in range(2):
            sums = (c, shard1(c, side), r1[c][side], *first[side])
            scatter_mid(RS1_OUT + side, RS1 + 2 * side, *sums)

    def sum_end(c):
        for side in range(2):
            halves = scatter_end(
                RS1 + 2 * side, c, shard1(c, side), r1[c][side], first[side][0]
            )
            for h in range(2):
                gf[c][side][h * 4 : (h + 1) * 4] = halves[h]
                gb[c][side][h * 4 : (h + 1) * 4] = halves[h].astype(jnp.bfloat16)
            index, ring = second[side]
            to_ring(
                RS2_OUT + side,
                (RS2 + side,) * 3,
                c,
                lambda step: gb[c][side].at[pl.ds(2 * mod4(index + step), 2)],
                lambda slot: r2[c][side].at[slot],
                index,
                ring,
            )

    def cross_end(c):
        for side in range(2):
            index, ring = second[side]
            total = gf[c][side][pl.ds(2 * index, 2)]
            arrived(r2[c][side], RS2 + side, c)
            for slot in range(3):
                total = total + f32(r2[c][side][slot])
            cols = columns(side, first[side][0])
            part2(c, side, index)[...] = (total * oscale[:, cols]).astype(jnp.bfloat16)
            own = part2(c, side, index)
            to_ring(
                AG2_OUT + side,
                (AG2 + side,) * 3,
                c,
                lambda step: own,
                lambda slot: own,
                index,
                ring,
            )

    def spread_end(c):
        for side in range(2):
            arrived(r2[c][side], AG2 + side, c)
            gather_start(AG1_OUT + side, AG1 + 2 * side, c, part1(c, side), *first[side])

    def last_mid(c):
        for side in range(2):
            spread = (c, part1(c, side), r1[c][side], *first[side])
            gather_mid(AG1_OUT + side, AG1 + 2 * side, *spread)

    def last_end(c):
        for side in range(2):
            gather_end(AG1 + 2 * side, c, r1[c][side])

    stages = (
        project,
        pair_cores,
        project_mid,
        project_end,
        attend,
        combine,
        gather_heads,
        output,
        sum_mid,
        sum_end,
        cross_end,
        spread_end,
        last_mid,
        last_end,
    )
    for c, i in ORDER:
        stages[i](c)

    for c in range(NC):
        departed(crecv.at[c], CORE_OUT, c)
        departed(landed.at[c, 0], SQC_OUT, c)
        departed(landed.at[c, pl.ds(1, 3)], SQZ_OUT, c)
        departed(zrecv.at[c], ZRS_OUT, c)
        departed(qbuf.at[c, 0], SWAP_OUT, c)
        departed(kvbuf.at[c, 0], SWAP_OUT + 1, c)
        departed(orecv.at[c], FAR_OUT, c)
        departed(trecv.at[c], TOPS_OUT, c)
        departed(gat.at[c, pl.ds(0, 3)], ZAG_OUT, c)
        departed(gat.at[c, pl.ds(0, 4)], CAG_OUT, c)
        for side in range(2):
            departed(r1[c][side], RS1_OUT + side, c)
            departed(r2[c][side], RS2_OUT + side, c)
            departed(r2[c][side], AG2_OUT + side, c)
            departed(r1[c][side], AG1_OUT + side, c)


def shards(
    states,
    lengths,
    norm_gain,
    query_weight,
    keyval_weight,
    output_weight,
    query_scale,
    keyval_scale,
    output_scale,
    key_cache,
    value_cache,
):
    table = rotary_table(HD)
    frequencies = jnp.concatenate([table, table])[None, :]
    bf16 = jnp.bfloat16
    vmem = pl.BlockSpec(memory_space=pltpu.VMEM)
    smem = pl.BlockSpec(memory_space=pltpu.SMEM)
    hbm = pl.BlockSpec(memory_space=pl.ANY)
    result = pl.pallas_call(
        kernel,
        out_shape=pltpu.VMEM((NB, ROWS_HERE * DRAFT, OUTS), bf16),
        in_specs=[smem] + [vmem] * 5 + [hbm] * 6,
        out_specs=vmem,
        scratch_shapes=[
            pltpu.VMEM((ROWS_HERE * DRAFT, HD), jnp.float32),
            pltpu.VMEM((ROWS_HERE * DRAFT, HD), jnp.float32),
            pltpu.VMEM((NC, NB, T, FEATS), bf16),
            pltpu.VMEM((FEATS, QW), bf16),
            pltpu.VMEM((FEATS, HD), bf16),
            pltpu.VMEM((QW, OUTS), bf16),
            pltpu.VMEM((ROWS_HERE, SPAN, HD), bf16),
            pltpu.VMEM((ROWS_HERE, SPAN, HD), bf16),
            pltpu.VMEM((M, FEATS), bf16),
            pltpu.VMEM((NC, 2, 4, T, WIDE), jnp.float32),
            pltpu.VMEM((NC, 4, T, WIDE), jnp.float32),
            pltpu.VMEM((NC, 6, T // 2, WIDE), jnp.float32),
            pltpu.VMEM((NC, 2, 1, M), jnp.float32),
            pltpu.VMEM((NC, 4, 1, M), jnp.float32),
            pltpu.VMEM((M, M), jnp.float32),
            pltpu.VMEM((NC, 2, CHUNK_ROWS, OWN * DRAFT, HD), bf16),
            pltpu.VMEM((NC, 2, T, HD), bf16),
            pltpu.VMEM((CHUNK_ROWS, HD, HD), bf16),
            pltpu.VMEM((CHUNK_ROWS, HD, HD), bf16),
            pltpu.VMEM((NC, 2, CHUNK_ROWS, HD, HD), jnp.float32),
            pltpu.VMEM((NC, 2, CHUNK_ROWS, HD, HD), bf16),
            pltpu.VMEM((NC, CHUNK_ROWS, HD, HD), bf16),
            pltpu.VMEM((NC, 2, CHUNK_ROWS, 8, HD), jnp.float32),
            pltpu.VMEM((NC, CHUNK_ROWS, 8, HD), jnp.float32),
            pltpu.VMEM((NC, NB, T, QW), bf16),
            pltpu.VMEM((NC, NB, T, OUTS), bf16),
            pltpu.SemaphoreType.DMA((NC + 5,)),
            pltpu.SemaphoreType.DMA((DEPARTURES, NC)),
            pltpu.SemaphoreType.DMA((ARRIVALS, NC)),
            *(
                shape
                for c in range(NC)
                for _ in range(2)
                for shape in (
                    pltpu.VMEM((6, 4, T, WIDTH), bf16),
                    pltpu.VMEM((NB, T, WIDTH), jnp.float32),
                    pltpu.VMEM((NB, T, WIDTH), bf16),
                    pltpu.VMEM((3, 2, T, WIDTH), bf16),
                )
            ),
        ],
        compiler_params=pltpu.CompilerParams(
            collective_id=0, has_side_effects=True, vmem_limit_bytes=LIMIT * 2**20
        ),
        cost_estimate=pl.CostEstimate(
            flops=12 * 10**9, bytes_accessed=25 * 2**20, transcendentals=2**22
        ),
    )(
        lengths,
        frequencies,
        norm_gain[None, :],
        query_scale[None, :],
        keyval_scale[None, :],
        output_scale[None, :],
        states.reshape(NB, ROWS_HERE * DRAFT, FEATS),
        query_weight,
        keyval_weight,
        output_weight,
        key_cache,
        value_cache,
    )
    return result.reshape(NB * ROWS_HERE * DRAFT, OUTS)


def solution(mesh):
    placed = (
        P(None, "din"),
        P("din"),
        P("din"),
        P("din", "dout"),
        P("din", "dout"),
        P("dout", "din"),
        P("dout"),
        P("dout"),
        P("din"),
        P("din", "dout", None),
        P("din", "dout", None),
    )
    return jax.shard_map(
        shards, mesh=mesh, in_specs=placed, out_specs=P(None, "din"), check_vma=False
    )
```

```python
import functools
import math

import jax
import jax.numpy as jnp
from jax import lax
from jax.experimental import pallas as pl
from jax.experimental.pallas import tpu as pltpu
from jax.sharding import PartitionSpec as P

D = 16384
HQ = 128
KVH = 8
HD = 128
DRAFT = 16
ROWS_HERE = 8
OWN = 8
QW = OWN * HD
WIDE = QW + HD
SPAN = 2048
TILE = 512
FEATS = 2048
OUTS = 2048

CHUNK_ROWS = 1
NC = ROWS_HERE // CHUNK_ROWS
T = CHUNK_ROWS * DRAFT
NB = 8
M = NB * T
LOG_SCALE = math.log2(math.e) / math.sqrt(HD)
LOWEST = -1e30
LIMIT = 56

WIDTH = OUTS // 8

CORE = 0
ZRS = 1
SWAP = 3
FAR = 5
TOPS = FAR + CHUNK_ROWS
ZAG = TOPS + CHUNK_ROWS
CAG = ZAG + 3
SQC = CAG + 1
SQZ = SQC + 1
RS1 = SQZ + 1
RS2 = RS1 + 4
AG2 = RS2 + 2
AG1 = AG2 + 2
ARRIVALS = AG1 + 4
CORE_OUT, ZRS_OUT, SWAP_OUT, FAR_OUT, ZAG_OUT, CAG_OUT = 0, 1, 2, 4, 5, 6
RS1_OUT, RS2_OUT, AG2_OUT, AG1_OUT, TOPS_OUT, SQC_OUT, SQZ_OUT = 7, 9, 11, 13, 15, 16, 17
DEPARTURES = 18

ORDER = (
    (0, 0), (1, 0), (0, 1), (3, 0), (1, 1), (2, 0), (7, 0), (3, 1), (4, 0), (0, 2),
    (1, 2), (5, 0), (2, 1), (3, 2), (4, 1), (0, 3), (1, 3), (2, 2), (5, 1), (6, 0),
    (3, 3), (4, 2), (6, 1), (0, 4), (2, 3), (5, 2), (7, 1), (1, 4), (3, 4), (4, 3),
    (6, 2), (0, 5), (5, 3), (2, 4), (7, 2), (1, 5), (3, 5), (6, 3), (4, 4), (0, 6),
    (5, 4), (2, 5), (7, 3), (0, 7), (1, 6), (6, 4), (3, 6), (1, 7), (5, 5), (7, 4),
    (2, 6), (4, 5), (0, 8), (3, 7), (2, 7), (6, 5), (5, 6), (1, 8), (7, 5), (0, 9),
    (4, 6), (5, 7), (2, 8), (4, 7), (6, 6), (7, 6), (0, 10), (3, 8), (7, 7), (6, 7),
    (1, 9), (5, 8), (3, 9), (2, 9), (4, 8), (0, 11), (5, 9), (6, 8), (3, 10), (1, 10),
    (4, 9), (7, 8), (0, 12), (2, 10), (5, 10), (6, 9), (4, 10), (7, 9), (1, 11), (5, 11),
    (4, 11), (7, 10), (6, 10), (0, 13), (2, 11), (3, 11), (5, 12), (6, 11), (7, 11), (2, 12),
    (1, 12), (4, 12), (3, 12), (6, 12), (7, 12), (3, 13), (6, 13), (4, 13), (1, 13), (5, 13),
    (2, 13), (7, 13),
)


def rotary_table(head_size):
    entries = []
    for index in range(head_size // 2):
        inverse = 1.0 / 500000.0 ** (2.0 * index / head_size)
        wavelength = 2.0 * math.pi / inverse
        smooth = min(max((8192.0 / wavelength - 1.0) / 3.0, 0.0), 1.0)
        entries.append((1.0 - smooth) * inverse / 8.0 + smooth * inverse)
    return jnp.asarray(entries, dtype=jnp.float32)


def mod4(v):
    return lax.rem(v, 4)


def f32(v):
    return v.astype(jnp.float32)


def kernel(
    lengths, frequencies, gain, qscale, kvscale, oscale,
    states, wq, wkv, wo, keys, values,
    out,
    cosines, sines,
    xs, wq_v, wkv_v, wo_v, k_v, v_v, scaled,
    ybuf, crecv, zrecv, squares, landed, inverses, qbuf, kvbuf, kpad, vpad, obuf, osend, orecv, tops, trecv, gat,
    pbuf,
    load_sem, send_sem, recv_sem,
    *sides,
):
    r1, gf, gb, r2 = (
        [[sides[4 * (2 * c + side) + kind] for side in range(2)] for c in range(NC)]
        for kind in range(4)
    )
    din = lax.axis_index("din")
    dout = lax.axis_index("dout")
    core = lax.rem(din, 2)
    z = lax.div(din, 2)
    x = lax.rem(dout, 4)
    y = lax.div(dout, 4)
    parity = lax.rem(x, 2)
    core_peer = (din + 1 - 2 * core, dout)
    pair_peer = (din, dout + 1 - 2 * parity)
    z_plus = (lax.rem(din + 2, 8), dout)
    z_minus = (lax.rem(din + 6, 8), dout)
    x_plus = (din, 4 * y + mod4(x + 1))
    x_minus = (din, 4 * y + mod4(x + 3))
    y_plus = (din, lax.rem(dout + 4, 16))
    y_minus = (din, lax.rem(dout + 12, 16))
    z_ring = (z_plus, (lax.rem(din + 4, 8), dout), z_minus)
    x_ring = (x_plus, (din, 4 * y + mod4(x + 2)), x_minus)
    y_ring = (y_plus, (din, lax.rem(dout + 8, 16)), y_minus)
    neighbours = (core_peer, *z_ring, *x_ring, *y_ring)

    def load(src, dst, index):
        return pltpu.make_async_copy(src, dst, load_sem.at[index])

    def states_load(c):
        return load(states.at[:, pl.ds(c * T, T), :], xs.at[c], c)

    wq_load = load(wq, wq_v, NC)
    wkv_load = load(wkv, wkv_v, NC + 1)
    wo_load = load(wo, wo_v, NC + 2)
    k_load = load(keys, k_v, NC + 3)
    v_load = load(values, v_v, NC + 4)
    states_load(0).start()
    wq_load.start()
    wkv_load.start()
    for c in range(1, NC):
        states_load(c).start()
    k_load.start()
    v_load.start()
    wo_load.start()

    barrier = pltpu.get_barrier_semaphore()
    for peer in neighbours:
        pl.semaphore_signal(barrier, inc=1, device_id=peer, device_id_type=pl.DeviceIdType.MESH)
    draft = lax.broadcasted_iota(jnp.int32, (DRAFT, HD), 0)
    sign = jnp.where(lax.broadcasted_iota(jnp.int32, (DRAFT, HD), 1) < HD // 2, -1.0, 1.0)
    for row in range(ROWS_HERE):
        angles = f32(draft + lengths[row]) * frequencies[...]
        place = pl.ds(row * DRAFT, DRAFT)
        cosines[place] = jnp.cos(angles)
        sines[place] = jnp.sin(angles) * sign
    pl.semaphore_wait(barrier, len(neighbours))

    def remote(src, dst, out_row, row, c, peer):
        return pltpu.make_async_remote_copy(
            src_ref=src,
            dst_ref=dst,
            send_sem=send_sem.at[out_row, c],
            recv_sem=recv_sem.at[row, c],
            device_id=peer,
            device_id_type=pl.DeviceIdType.MESH,
        )

    def send(src, dst, out_row, row, c, peer):
        remote(src, dst, out_row, row, c, peer).start()

    def arrived(like, row, c):
        remote(like, like, 0, row, c, core_peer).wait_recv()

    def departed(like, out_row, c):
        remote(like, like, out_row, 0, c, core_peer).wait_send()

    def scatter_start(out_row, row, c, shard, land, index, plus, minus):
        far = mod4(index + 2)
        send(shard(far, 1), land.at[0], out_row, row, c, plus)
        send(shard(far, 0), land.at[1], out_row, row, c, minus)
        send(shard(mod4(index + 1), 0), land.at[2], out_row, row + 1, c, plus)
        send(shard(mod4(index + 3), 1), land.at[3], out_row, row + 1, c, minus)

    def scatter_mid(out_row, row, c, shard, land, index, plus, minus):
        arrived(land.at[pl.ds(0, 2)], row, c)
        for slot, step, half, peer in ((0, 1, 1, plus), (1, 3, 0, minus)):
            piece = shard(mod4(index + step), half)
            piece[...] = (f32(piece[...]) + f32(land[slot])).astype(piece.dtype)
            send(piece, land.at[4 + slot], out_row, row + 1, c, peer)

    def to_ring(out_row, rows, c, part, land, index, peers):
        for slot in (1, 0, 2):
            send(part(slot + 1), land(slot), out_row, rows[slot], c, peers[slot])

    def scatter_end(row, c, shard, land, index):
        arrived(land.at[pl.ds(2, 4)], row + 1, c)
        return [
            f32(shard(index, half)[...]) + f32(land[direct]) + f32(land[chained])
            for half, direct, chained in ((0, 2, 5), (1, 3, 4))
        ]

    def gather_start(out_row, row, c, part, index, plus, minus):
        own = part(index, None)
        send(own, own, out_row, row, c, plus)
        send(own, own, out_row, row, c, minus)

    def gather_mid(out_row, row, c, part, like, index, plus, minus):
        arrived(like.at[pl.ds(0, 4)], row, c)
        for step, half, peer in ((3, 0, plus), (1, 1, minus)):
            piece = part(mod4(index + step), half)
            send(piece, piece, out_row, row + 1, c, peer)

    def gather_end(row, c, like):
        arrived(like.at[pl.ds(0, 2)], row + 1, c)

    def project(c):
        states_load(c).wait()
        wide = f32(xs[c]).reshape(M, FEATS)
        column = jnp.sum(wide * wide, axis=1, keepdims=True)
        squares[c, 0] = jnp.broadcast_to(column, (M, M)).T[0:1]
        send(squares.at[c, 0], landed.at[c, 0], SQC_OUT, SQC, c, core_peer)
        scaled[...] = (wide * gain[...]).astype(jnp.bfloat16)
        if c == 0:
            wq_load.wait()
            wkv_load.wait()

        def put(block, start):
            for b in range(NB):
                ybuf[c, b % 2, b // 2, :, start] = block[b * T : (b + 1) * T]

        put(
            jnp.dot(scaled[...], wkv_v[...], preferred_element_type=jnp.float32), pl.ds(QW, HD)
        )

        put(jnp.dot(scaled[...], wq_v[...], preferred_element_type=jnp.float32), pl.ds(0, QW))
        send(ybuf.at[c, 1 - core], crecv.at[c], CORE_OUT, CORE, c, core_peer)

    def z_shard(c):
        return lambda t, h: ybuf.at[c, core, t, pl.ds(h * (T // 2), T // 2), :]

    def pair_cores(c):
        arrived(crecv.at[c], CORE, c)
        ybuf[c, core] = ybuf[c, core] + crecv[c]
        scatter_start(ZRS_OUT, ZRS, c, z_shard(c), zrecv.at[c], z, z_plus, z_minus)
        arrived(landed.at[c, 0], SQC, c)
        squares[c, 1] = squares[c, 0] + landed[c, 0]
        own = squares.at[c, 1]
        to_ring(
            SQZ_OUT, (SQZ,) * 3, c, lambda step: own, lambda k: landed.at[c, k + 1], z, z_ring
        )

    def project_mid(c):
        scatter_mid(ZRS_OUT, ZRS, c, z_shard(c), zrecv.at[c], z, z_plus, z_minus)

    def project_end(c):
        total = jnp.concatenate(scatter_end(ZRS, c, z_shard(c), zrecv.at[c], z), axis=0)
        arrived(landed.at[c, pl.ds(1, 3)], SQZ, c)
        summed = squares[c, 1] + landed[c, 1] + landed[c, 2] + landed[c, 3]
        row = lax.rsqrt(summed / D + 1e-05)
        inverses[...] = jnp.broadcast_to(row, (M, M)).T
        inverse = inverses[pl.ds(pl.multiple_of(din * T, T), T)]
        cosine = cosines[c * T : (c + 1) * T]
        sine = sines[c * T : (c + 1) * T]
        half = HD // 2
        for h in range(OWN):
            cols = slice(h * HD, (h + 1) * HD)
            raw = total[:, cols] * qscale[:, cols] * inverse
            turned = jnp.concatenate([raw[:, half:], raw[:, :half]], axis=1)
            query = (raw * cosine + turned * sine).astype(jnp.bfloat16)
            for r in range(CHUNK_ROWS):
                qbuf[c, parity, r, pl.ds(h * DRAFT, DRAFT), :] = query[
                    r * DRAFT : (r + 1) * DRAFT
                ]
        raw = total[:, QW : QW + HD] * kvscale[...] * inverse
        turned = jnp.concatenate([raw[:, half:], raw[:, :half]], axis=1)
        rotated = raw * cosine + turned * sine
        kvbuf[c, parity] = jnp.where(parity == 0, rotated, raw).astype(jnp.bfloat16)
        send(qbuf.at[c, parity], qbuf.at[c, parity], SWAP_OUT, SWAP, c, pair_peer)
        send(kvbuf.at[c, parity], kvbuf.at[c, parity], SWAP_OUT + 1, SWAP + 1, c, pair_peer)

    def attend(c):
        if c == 0:
            kpad[...] = jnp.zeros_like(kpad)
            vpad[...] = jnp.zeros_like(vpad)
            k_load.wait()
            v_load.wait()
        arrived(qbuf.at[c, 1 - parity], SWAP, c)
        arrived(kvbuf.at[c, 1 - parity], SWAP + 1, c)
        place = lax.broadcasted_iota(jnp.int32, (1, SPAN), 1) + parity * SPAN
        token = lax.rem(lax.broadcasted_iota(jnp.int32, (2 * OWN * DRAFT, HD), 0), DRAFT)
        other = lax.broadcasted_iota(jnp.int32, (2 * OWN * DRAFT, HD), 1)
        drafted = (other <= token) & (parity == 0)
        lane = lax.broadcasted_iota(jnp.int32, (QW // OWN, HD), 1)
        for r in range(CHUNK_ROWS):
            row = c * CHUNK_ROWS + r
            kpad[r, 0:DRAFT] = kvbuf[c, 0, r * DRAFT : (r + 1) * DRAFT]
            vpad[r, 0:DRAFT] = kvbuf[c, 1, r * DRAFT : (r + 1) * DRAFT]
            query = jnp.concatenate([qbuf[c, 0, r], qbuf[c, 1, r]], axis=0)
            across = (((1,), (1,)), ((), ()))
            bias = jnp.where(place < lengths[row], 0.0, LOWEST)
            tiles = [slice(i * TILE, (i + 1) * TILE) for i in range(SPAN // TILE)]
            fresh = lax.dot_general(
                query, kpad[r], across, preferred_element_type=jnp.float32
            )
            fresh = jnp.where(drafted, fresh * LOG_SCALE, LOWEST)
            top = jnp.max(fresh, axis=1, keepdims=True)
            scores = []
            for tile in tiles:
                part = lax.dot_general(
                    query, k_v[row, tile], across, preferred_element_type=jnp.float32
                )
                scores.append(part * LOG_SCALE + bias[:, tile])
                top = jnp.maximum(top, jnp.max(scores[-1], axis=1, keepdims=True))
            weights = jnp.exp2(fresh - top)
            totals = jnp.sum(weights, axis=1, keepdims=True)
            weighted = jnp.dot(
                weights.astype(jnp.bfloat16), vpad[r], preferred_element_type=jnp.float32
            )
            for tile, part in zip(tiles, scores):
                weights = jnp.exp2(part - top)
                totals = totals + jnp.sum(weights, axis=1, keepdims=True)
                weighted = weighted + jnp.dot(
                    weights.astype(jnp.bfloat16), v_v[row, tile], preferred_element_type=jnp.float32
                )
            for p in range(2):
                mine = slice(p * QW // OWN, (p + 1) * QW // OWN)
                both = jnp.where(lane < HD // 2, top[mine], totals[mine]).T
                obuf[c, p, r] = weighted[mine]
                osend[c, p, r] = weighted[mine].astype(jnp.bfloat16)
                tops[c, p, r, 0:4] = both[0:4]
                tops[c, p, r, 4:8] = both[HD // 2 : HD // 2 + 4]
            far = 1 - parity
            send(tops.at[c, far, r], trecv.at[c, r], TOPS_OUT, TOPS + r, c, pair_peer)
            send(osend.at[c, far, r], orecv.at[c, r], FAR_OUT, FAR + r, c, pair_peer)

    def to_core(c, t):
        block = gat.at[c, 2 * t + core]
        send(block, block, CAG_OUT, CAG, c, core_peer)

    def combine(c):
        for r in range(CHUNK_ROWS):
            arrived(trecv.at[c, r], TOPS + r, c)
            arrived(orecv.at[c, r], FAR + r, c)
            near_top, near_total = tops[c, parity, r, 0:4], tops[c, parity, r, 4:8]
            far_top, far_total = trecv[c, r, 0:4], trecv[c, r, 4:8]
            joint = jnp.maximum(near_top, far_top)
            near_factor = jnp.exp2(near_top - joint)
            far_factor = jnp.exp2(far_top - joint)
            share = 1.0 / (near_total * near_factor + far_total * far_factor)

            def spread(factor):
                return jnp.broadcast_to((factor * share)[0:1], (HD, HD)).T

            heads = (
                obuf[c, parity, r] * spread(near_factor)
                + f32(orecv[c, r]) * spread(far_factor)
            ).astype(jnp.bfloat16)
            for h in range(OWN):
                gat[c, din, r * DRAFT : (r + 1) * DRAFT, h * HD : (h + 1) * HD] = heads[
                    h * DRAFT : (h + 1) * DRAFT
                ]
        own = gat.at[c, din]
        rows = (ZAG, ZAG + 1, ZAG + 2)
        to_ring(ZAG_OUT, rows, c, lambda step: own, lambda slot: own, z, z_ring)
        to_core(c, z)

    def gather_heads(c):
        for slot in (0, 2, 1):
            t = mod4(z + 3 - slot)
            arrived(gat.at[c, 2 * t + core], ZAG + slot, c)
            to_core(c, t)

    first = ((x, x_plus, x_minus), (y, y_plus, y_minus))
    second = ((y, y_ring), (x, x_ring))

    def columns(side, t):
        return pl.ds(pl.multiple_of((4 * side + t) * WIDTH, WIDTH), WIDTH)

    def rows(c):
        return pl.ds(c * T, T)

    def shard1(c, side):
        return lambda t, h: pbuf.at[c, pl.ds(h * 4, 4), :, columns(side, t)]

    def part2(c, side, t):
        return out.at[pl.ds(2 * t, 2), rows(c), columns(side, first[side][0])]

    def part1(c, side):
        def part(t, half):
            if half is None:
                return out.at[:, rows(c), columns(side, t)]
            return out.at[pl.ds(half * 4, 4), rows(c), columns(side, t)]

        return part

    def output(c):
        if c == 0:
            wo_load.wait()
        arrived(gat.at[c, pl.ds(0, 4)], CAG, c)

        heads = gat[c].reshape(M, QW)
        for side in (1, 0):
            width = OUTS // 2
            cols = slice(side * width, (side + 1) * width)
            block = jnp.dot(heads, wo_v[:, cols], preferred_element_type=jnp.float32)
            pbuf[c, :, :, cols] = block.astype(jnp.bfloat16).reshape(NB, T, width)
            sums = (c, shard1(c, side), r1[c][side], *first[side])
            scatter_start(RS1_OUT + side, RS1 + 2 * side, *sums)

    def sum_mid(c):
        for side in range(2):
            sums = (c, shard1(c, side), r1[c][side], *first[side])
            scatter_mid(RS1_OUT + side, RS1 + 2 * side, *sums)

    def sum_end(c):
        for side in range(2):
            halves = scatter_end(
                RS1 + 2 * side, c, shard1(c, side), r1[c][side], first[side][0]
            )
            for h in range(2):
                gf[c][side][h * 4 : (h + 1) * 4] = halves[h]
                gb[c][side][h * 4 : (h + 1) * 4] = halves[h].astype(jnp.bfloat16)
            index, ring = second[side]
            to_ring(
                RS2_OUT + side,
                (RS2 + side,) * 3,
                c,
                lambda step: gb[c][side].at[pl.ds(2 * mod4(index + step), 2)],
                lambda slot: r2[c][side].at[slot],
                index,
                ring,
            )

    def cross_end(c):
        for side in range(2):
            index, ring = second[side]
            total = gf[c][side][pl.ds(2 * index, 2)]
            arrived(r2[c][side], RS2 + side, c)
            for slot in range(3):
                total = total + f32(r2[c][side][slot])
            cols = columns(side, first[side][0])
            part2(c, side, index)[...] = (total * oscale[:, cols]).astype(jnp.bfloat16)
            own = part2(c, side, index)
            to_ring(
                AG2_OUT + side,
                (AG2 + side,) * 3,
                c,
                lambda step: own,
                lambda slot: own,
                index,
                ring,
            )

    def spread_end(c):
        for side in range(2):
            arrived(r2[c][side], AG2 + side, c)
            gather_start(AG1_OUT + side, AG1 + 2 * side, c, part1(c, side), *first[side])

    def last_mid(c):
        for side in range(2):
            spread = (c, part1(c, side), r1[c][side], *first[side])
            gather_mid(AG1_OUT + side, AG1 + 2 * side, *spread)

    def last_end(c):
        for side in range(2):
            gather_end(AG1 + 2 * side, c, r1[c][side])

    stages = (
        project,
        pair_cores,
        project_mid,
        project_end,
        attend,
        combine,
        gather_heads,
        output,
        sum_mid,
        sum_end,
        cross_end,
        spread_end,
        last_mid,
        last_end,
    )
    for c, i in ORDER:
        stages[i](c)

    for c in range(NC):
        departed(crecv.at[c], CORE_OUT, c)
        departed(landed.at[c, 0], SQC_OUT, c)
        departed(landed.at[c, pl.ds(1, 3)], SQZ_OUT, c)
        departed(zrecv.at[c], ZRS_OUT, c)
        departed(qbuf.at[c, 0], SWAP_OUT, c)
        departed(kvbuf.at[c, 0], SWAP_OUT + 1, c)
        departed(orecv.at[c], FAR_OUT, c)
        departed(trecv.at[c], TOPS_OUT, c)
        departed(gat.at[c, pl.ds(0, 3)], ZAG_OUT, c)
        departed(gat.at[c, pl.ds(0, 4)], CAG_OUT, c)
        for side in range(2):
            departed(r1[c][side], RS1_OUT + side, c)
            departed(r2[c][side], RS2_OUT + side, c)
            departed(r2[c][side], AG2_OUT + side, c)
            departed(r1[c][side], AG1_OUT + side, c)


def shards(
    states,
    lengths,
    norm_gain,
    query_weight,
    keyval_weight,
    output_weight,
    query_scale,
    keyval_scale,
    output_scale,
    key_cache,
    value_cache,
):
    table = rotary_table(HD)
    frequencies = jnp.concatenate([table, table])[None, :]
    bf16 = jnp.bfloat16
    vmem = pl.BlockSpec(memory_space=pltpu.VMEM)
    smem = pl.BlockSpec(memory_space=pltpu.SMEM)
    hbm = pl.BlockSpec(memory_space=pl.ANY)
    result = pl.pallas_call(
        kernel,
        out_shape=pltpu.VMEM((NB, ROWS_HERE * DRAFT, OUTS), bf16),
        in_specs=[smem] + [vmem] * 5 + [hbm] * 6,
        out_specs=vmem,
        scratch_shapes=[
            pltpu.VMEM((ROWS_HERE * DRAFT, HD), jnp.float32),
            pltpu.VMEM((ROWS_HERE * DRAFT, HD), jnp.float32),
            pltpu.VMEM((NC, NB, T, FEATS), bf16),
            pltpu.VMEM((FEATS, QW), bf16),
            pltpu.VMEM((FEATS, HD), bf16),
            pltpu.VMEM((QW, OUTS), bf16),
            pltpu.VMEM((ROWS_HERE, SPAN, HD), bf16),
            pltpu.VMEM((ROWS_HERE, SPAN, HD), bf16),
            pltpu.VMEM((M, FEATS), bf16),
            pltpu.VMEM((NC, 2, 4, T, WIDE), jnp.float32),
            pltpu.VMEM((NC, 4, T, WIDE), jnp.float32),
            pltpu.VMEM((NC, 6, T // 2, WIDE), jnp.float32),
            pltpu.VMEM((NC, 2, 1, M), jnp.float32),
            pltpu.VMEM((NC, 4, 1, M), jnp.float32),
            pltpu.VMEM((M, M), jnp.float32),
            pltpu.VMEM((NC, 2, CHUNK_ROWS, OWN * DRAFT, HD), bf16),
            pltpu.VMEM((NC, 2, T, HD), bf16),
            pltpu.VMEM((CHUNK_ROWS, HD, HD), bf16),
            pltpu.VMEM((CHUNK_ROWS, HD, HD), bf16),
            pltpu.VMEM((NC, 2, CHUNK_ROWS, HD, HD), jnp.float32),
            pltpu.VMEM((NC, 2, CHUNK_ROWS, HD, HD), bf16),
            pltpu.VMEM((NC, CHUNK_ROWS, HD, HD), bf16),
            pltpu.VMEM((NC, 2, CHUNK_ROWS, 8, HD), jnp.float32),
            pltpu.VMEM((NC, CHUNK_ROWS, 8, HD), jnp.float32),
            pltpu.VMEM((NC, NB, T, QW), bf16),
            pltpu.VMEM((NC, NB, T, OUTS), bf16),
            pltpu.SemaphoreType.DMA((NC + 5,)),
            pltpu.SemaphoreType.DMA((DEPARTURES, NC)),
            pltpu.SemaphoreType.DMA((ARRIVALS, NC)),
            *(
                shape
                for c in range(NC)
                for _ in range(2)
                for shape in (
                    pltpu.VMEM((6, 4, T, WIDTH), bf16),
                    pltpu.VMEM((NB, T, WIDTH), jnp.float32),
                    pltpu.VMEM((NB, T, WIDTH), bf16),
                    pltpu.VMEM((3, 2, T, WIDTH), bf16),
                )
            ),
        ],
        compiler_params=pltpu.CompilerParams(
            collective_id=0, has_side_effects=True, vmem_limit_bytes=LIMIT * 2**20
        ),
        cost_estimate=pl.CostEstimate(
            flops=12 * 10**9, bytes_accessed=25 * 2**20, transcendentals=2**22
        ),
    )(
        lengths,
        frequencies,
        norm_gain[None, :],
        query_scale[None, :],
        keyval_scale[None, :],
        output_scale[None, :],
        states.reshape(NB, ROWS_HERE * DRAFT, FEATS),
        query_weight,
        keyval_weight,
        output_weight,
        key_cache,
        value_cache,
    )
    return result.reshape(NB * ROWS_HERE * DRAFT, OUTS)


def solution(mesh):
    placed = (
        P(None, "din"),
        P("din"),
        P("din"),
        P("din", "dout"),
        P("din", "dout"),
        P("dout", "din"),
        P("dout"),
        P("dout"),
        P("din"),
        P("din", "dout", None),
        P("din", "dout", None),
    )
    return jax.shard_map(
        shards, mesh=mesh, in_specs=placed, out_specs=P(None, "din"), check_vma=False
    )
```
